256 devices in a mesh: region: 16 (over z, x_hi), group: 16 (over y, x_lo, core).
Axes of the slice: x: 4 (x_hi: 2, x_lo: 2; x = x_hi * 2 + x_lo), y: 4, z: 8, core: 2. Of those that a mesh axis runs over, the one named last changes fastest.
Arguments:
- nodes: bfloat16 [65536, 512], P(('region', 'group')), may hold values from -6 to 6
- coarse: bfloat16 [512, 512], P(('region', 'group')), may hold values from -6 to 6
- edges: bfloat16 [393216, 512], P(('region', 'group')), may hold values from -6 to 6
- senders: int32 [393216], P(('region', 'group')), may hold values from 0 to 1279, as said below
- receivers: int32 [393216], P(('region', 'group')), may hold values from 0 to 127
- counts: int32 [512], P(('region', 'group')), may hold values from 96 to 768, as said below
- edge_in: bfloat16 [1536, 512], replicated, may hold values from -0.15625 to 0.15625
- edge_out: bfloat16 [512, 512], replicated, may hold values from -0.25 to 0.25
- edge_gain: float32 [512], replicated, may hold values from 0.1 to 1.9
- edge_shift: float32 [512], replicated, may hold values from -1.2 to 1.2
- node_in: bfloat16 [1024, 512], replicated, may hold values from -0.1875 to 0.1875
- node_out: bfloat16 [512, 512], replicated, may hold values from -0.25 to 0.25
- node_gain: float32 [512], replicated, may hold values from 0.1 to 1.9
- node_shift: float32 [512], replicated, may hold values from -3 to 3
Outputs:
- new_nodes: bfloat16 [65536, 512], P(('region', 'group'))
- new_coarse: bfloat16 [512, 512], P(('region', 'group'))
- new_edges: bfloat16 [393216, 512], P(('region', 'group'))
The draws below stay inside these ranges and needn't reach their ends.
Inputs may be any that keep to these rules, and one draw needn't show every extreme that they name: `senders`: A sender below 256 never stands on a device of region 0, and one from 512 to 767 never on a device of the last region. `counts`: every device has a block with 768 live edges.
All inputs are finite; a program needn't handle non-finite values.
Results may differ from the reference program's by a relative error of at most 0.007.
Values may be sent and summed in bfloat16 or wider, within the bound.
No kernel may reach another device: no remote copies, remote signals or barrier semaphores. Data moves between devices by JAX's collectives and lax.ppermute only.
A program may use at most 64 MiB of HBM per device.

```python
import jax
import jax.numpy as jnp
from jax import lax

D = 512
BLK = 128
CAP = 768
NB = 2
C_DEV = 2
REGIONS = 16
GROUPS = 16
SHARDS = 256
NODES = 256
EDGES_DEV = 1536
NODES_ALL = 65536
COARSE = 512
EDGES = 393216
BLOCKS = 512


def draw_senders(key, part):
    key = jax.random.fold_in(key, 11)
    key_kind, key_local, key_coarse, key_pick, key_near = jax.random.split(key, 5)
    slot_ids = jnp.arange(EDGES, dtype=jnp.int32)
    device = slot_ids // EDGES_DEV
    region_index = device // GROUPS
    kind = jax.random.randint(key_kind, (EDGES,), 0, 8, dtype=jnp.int32)
    local = jax.random.randint(key_local, (EDGES,), 0, NODES, dtype=jnp.int32)
    side = jnp.where(kind == 0, 0, jnp.where(kind == 1, 2, 1))
    side = jnp.where((side == 0) & (region_index == 0), 1, side)
    side = jnp.where((side == 2) & (region_index == REGIONS - 1), 1, side)
    spread_id = jax.random.randint(key_coarse, (EDGES,), 0, COARSE, dtype=jnp.int32)
    partner = (device + SHARDS // 2) % SHARDS
    near_id = partner * C_DEV + jax.random.randint(key_near, (EDGES,), 0, C_DEV, dtype=jnp.int32)
    pick = jax.random.randint(key_pick, (EDGES,), 0, 2, dtype=jnp.int32)
    coarse_id = jnp.where(pick == 0, near_id, spread_id)
    is_coarse = (kind >= 2) & (kind <= 4)
    result = jnp.where(is_coarse, 3 * NODES + coarse_id, side * NODES + local).astype(jnp.int32)
    result = result.at[EDGES_DEV * GROUPS].set(0)
    result = result.at[EDGES - 1].set(3 * NODES + COARSE - 1)
    return result


def draw_counts(key, part):
    key = jax.random.fold_in(key, 12)
    key_heavy, key_high, key_low, key_full = jax.random.split(key, 4)
    block_ids = jnp.arange(BLOCKS, dtype=jnp.int32)
    device = block_ids // NB
    heavy = jax.random.randint(key_heavy, (SHARDS,), 0, 4, dtype=jnp.int32) == 0
    high = jax.random.randint(key_high, (BLOCKS,), 3 * CAP // 4, CAP + 1, dtype=jnp.int32)
    low = jax.random.randint(key_low, (BLOCKS,), CAP // 8, CAP // 2 + 1, dtype=jnp.int32)
    result = jnp.where(jnp.take(heavy, device), high, low)
    full_block = jax.random.randint(key_full, (SHARDS,), 0, NB, dtype=jnp.int32)
    result = jnp.where(block_ids % NB == jnp.take(full_block, device), CAP, result)
    fewest = (jnp.take(full_block, jnp.zeros((1,), jnp.int32))[0] + 1) % NB
    result = jnp.where(block_ids == fewest, CAP // 8, result)
    return result.astype(jnp.int32)


def plant(entries, rng, low, high):
    place = [jax.random.randint(jax.random.fold_in(rng, axis), (), 0, length) for axis, length in enumerate(entries.shape)]
    main_axis = entries.shape.index(max(entries.shape))
    beside = place[:main_axis] + [(place[main_axis] + 1) % entries.shape[main_axis]] + place[main_axis + 1:]
    return entries.at[tuple(place)].set(low).at[tuple(beside)].set(high)


def levels(stream_key, extent, pieces, smallest, top_value):
    def one(axis_at, parts):
        heights = jax.random.uniform(jax.random.fold_in(jax.random.fold_in(stream_key, 6), axis_at), (parts,), jnp.float32, smallest / len(pieces), top_value / len(pieces))
        return jnp.repeat(jnp.exp(heights), extent[axis_at] // parts).reshape((-1,) + (1,) * (len(extent) - axis_at - 1))

    level = one(*pieces[0])
    for cut in pieces[1:]:
        level = level * one(*cut)
    return level


def scatter_about(own_key, extent, scale, bound, cuts=(), kind=jnp.bfloat16):
    array = scale * jax.random.normal(own_key, extent, jnp.float32)
    if cuts:
        array = array * levels(own_key, extent, cuts, -0.22, 0.18)
    return jnp.clip(array, -bound, bound).astype(kind)


def setup_inputs(seed: int = 0) -> dict:
    splits = jax.random.split(jax.random.key(seed), 15)
    nodes = scatter_about(splits[0], (NODES_ALL, D), 1.0, 6.0, ((0, 256),))
    coarse = scatter_about(splits[1], (COARSE, D), 1.0, 6.0, ((0, 256),))
    edges = scatter_about(splits[2], (EDGES, D), 1.0, 6.0, ((0, 256),))
    senders = draw_senders(jax.random.fold_in(splits[14], 71), 0)
    receivers = plant(jax.random.randint(splits[4], (EDGES,), 0, BLK), jax.random.fold_in(splits[4], 1), 0, BLK - 1).astype(jnp.int32)
    counts = draw_counts(jax.random.fold_in(splits[14], 71), 0)
    edge_in = scatter_about(splits[6], (3 * D, D), (3 * D) ** -0.5, 0.15625)
    edge_out = scatter_about(splits[7], (D, D), D ** -0.5, 0.25)
    edge_gain = jnp.clip(1.0 + 0.18 * jax.random.normal(splits[8], (D,), jnp.float32), 0.1, 1.9)
    edge_shift = scatter_about(splits[9], (D,), 0.2, 1.2, (), jnp.float32)
    node_in = scatter_about(splits[10], (2 * D, D), (2 * D) ** -0.5, 0.1875)
    node_out = scatter_about(splits[11], (D, D), D ** -0.5, 0.25)
    node_gain = jnp.clip(1.0 + 0.18 * jax.random.normal(splits[12], (D,), jnp.float32), 0.1, 1.9)
    node_shift = scatter_about(splits[13], (D,), 0.5, 3.0, (), jnp.float32)
    return dict(nodes=nodes, coarse=coarse, edges=edges, senders=senders, receivers=receivers, counts=counts, edge_in=edge_in, edge_out=edge_out, edge_gain=edge_gain, edge_shift=edge_shift, node_in=node_in, node_out=node_out, node_gain=node_gain, node_shift=node_shift)


def apply_mlp(inputs, w_in, w_out, ln_gain, ln_shift):
    hidden = jax.nn.silu(jnp.dot(inputs, w_in, preferred_element_type=jnp.float32)).astype(jnp.bfloat16)
    output = jnp.dot(hidden, w_out, preferred_element_type=jnp.float32)
    center = output - lax.optimization_barrier(jnp.mean(output, axis=-1, keepdims=True))
    spread = lax.optimization_barrier(jnp.mean(center * center, axis=-1, keepdims=True))
    return center * lax.rsqrt(spread + 1e-05) * ln_gain + ln_shift

def reference(nodes, coarse, edges, senders, receivers, counts, edge_in, edge_out, edge_gain, edge_shift, node_in, node_out, node_gain, node_shift):
    table = jnp.concatenate([nodes, coarse], axis=0)

    def device_step(coarse_acc, device):
        edge_start = (device * EDGES_DEV).astype(jnp.int32)
        edge_rows = lax.dynamic_slice_in_dim(edges, edge_start, EDGES_DEV, 0)
        send_ids = lax.dynamic_slice_in_dim(senders, edge_start, EDGES_DEV, 0)
        recv_ids = lax.dynamic_slice_in_dim(receivers, edge_start, EDGES_DEV, 0)
        block_counts = lax.dynamic_slice_in_dim(counts, (device * NB).astype(jnp.int32), NB, 0)
        own_nodes = lax.dynamic_slice_in_dim(nodes, (device * NODES).astype(jnp.int32), NODES, 0)
        side = send_ids // NODES
        fine_index = (device + (side - 1) * GROUPS) * NODES + send_ids % NODES
        glob_index = jnp.where(send_ids < 3 * NODES, fine_index, NODES_ALL + send_ids - 3 * NODES).astype(jnp.int32)
        send_rows = jnp.take(table, glob_index, axis=0)
        slot_ids = jnp.arange(EDGES_DEV, dtype=jnp.int32)
        block_of = slot_ids // CAP
        recv_local = (block_of * BLK + recv_ids).astype(jnp.int32)
        recv_rows = jnp.take(own_nodes, recv_local, axis=0)
        live = slot_ids % CAP < jnp.take(block_counts, block_of)
        joined = jnp.concatenate([edge_rows, send_rows, recv_rows], axis=-1)
        updated = (edge_rows.astype(jnp.float32) + apply_mlp(joined, edge_in, edge_out, edge_gain, edge_shift)).astype(jnp.bfloat16)
        new_rows = jnp.where(live[:, None], updated, edge_rows)
        masked = jnp.where(live[:, None], new_rows.astype(jnp.float32), jnp.float32(0.0))
        fine_sum = jax.ops.segment_sum(masked, recv_local, num_segments=NODES).astype(jnp.bfloat16)
        node_input = jnp.concatenate([own_nodes, fine_sum], axis=-1)
        node_new = (own_nodes.astype(jnp.float32) + apply_mlp(node_input, node_in, node_out, node_gain, node_shift)).astype(jnp.bfloat16)
        coarse_ids = jnp.where(live & (send_ids >= 3 * NODES), send_ids - 3 * NODES, COARSE).astype(jnp.int32)
        coarse_terms = jax.ops.segment_sum(masked, coarse_ids, num_segments=COARSE + 1)[:COARSE]
        return (coarse_acc + coarse_terms, (new_rows, node_new))
    coarse_acc, (edge_parts, node_parts) = lax.scan(device_step, jnp.zeros((COARSE, D), jnp.float32), jnp.arange(SHARDS, dtype=jnp.int32))
    coarse_input = jnp.concatenate([coarse, coarse_acc.astype(jnp.bfloat16)], axis=-1)
    new_coarse = (coarse.astype(jnp.float32) + apply_mlp(coarse_input, node_in, node_out, node_gain, node_shift)).astype(jnp.bfloat16)
    new_nodes = node_parts.reshape(NODES_ALL, D)
    new_edges = edge_parts.reshape(EDGES, D)
    return (new_nodes, new_coarse, new_edges)
```

```python
import jax
import jax.numpy as jnp
from jax import lax
from jax.experimental import pallas as pl
from jax.experimental.pallas import tpu as pltpu
from jax.sharding import Mesh, PartitionSpec as P

F32 = jnp.float32
BF16 = jnp.bfloat16
LANES = 128
VMEM_LIMIT = 48 * 1024 * 1024


def dot(a, b):
    return jnp.dot(a, b, preferred_element_type=F32)


def silu(x):
    return x / (1.0 + jnp.exp(-x))


def normed(output, gain, shift):
    center = output - jnp.mean(output, axis=-1, keepdims=True)
    spread = jnp.mean(center * center, axis=-1, keepdims=True)
    return center * lax.rsqrt(spread + 1e-05) * gain + shift


def columns_of(ids_ref, first, count):
    parts = []
    for k in range(count):
        row = ids_ref[pl.ds(first + k, 1), :].astype(F32)
        parts.append(jnp.broadcast_to(row, (LANES, LANES)).T)
    return jnp.concatenate(parts, axis=0)


def rows_of(ids_ref, first, count):
    return jnp.concatenate([ids_ref[pl.ds(first + k, 1), :] for k in range(count)], axis=1)


def pick_rows(column, width, offset=0):
    lane = lax.broadcasted_iota(jnp.int32, column.shape, 1).astype(F32)
    parts = [
        (column == lane + float(offset + k * LANES)).astype(F32).astype(BF16)
        for k in range(width // LANES)
    ]
    return jnp.concatenate(parts, axis=1)


def gather_kernel(
    senders_ref, receivers_ref, edges_ref, low_ref, nodes_ref, high_ref, w_in_ref, out_ref
):
    block = pl.program_id(0)
    slots, latent = edges_ref.shape
    node_rows = nodes_ref.shape[0]
    block_size = node_rows // pl.num_programs(0)
    chunks = slots // LANES
    send = columns_of(senders_ref, block * chunks, chunks)
    sent = (
        dot(pick_rows(send, node_rows), low_ref[...])
        + dot(pick_rows(send, node_rows, node_rows), nodes_ref[...])
        + dot(pick_rows(send, node_rows, 2 * node_rows), high_ref[...])
    ).astype(BF16)
    recv = columns_of(receivers_ref, block * chunks, chunks)
    own = nodes_ref[pl.ds(pl.multiple_of(block * 128, 128), 128), :]
    received = dot(pick_rows(recv, 128), own).astype(BF16)
    out_ref[...] = (
        dot(edges_ref[...], w_in_ref[:latent, :])
        + dot(sent, w_in_ref[latent : 2 * latent, :])
        + dot(received, w_in_ref[2 * latent :, :])
    )


def edge_kernel(
    counts_ref,
    places_ref,
    before_ref,
    edges_ref,
    mine_ref,
    other_ref,
    w_mid_ref,
    w_out_ref,
    gain_ref,
    shift_ref,
    new_edges_ref,
    to_mine_ref,
    to_other_ref,
    table,
    spread_rows,
    total,
):
    block = pl.program_id(0)
    slots, latent = edges_ref.shape
    chunks = slots // LANES
    quarters = latent // LANES
    half = mine_ref.shape[0] // quarters

    @pl.when(block == 0)
    def _():
        for side, ref in enumerate((mine_ref, other_ref)):
            spread_rows[...] = ref[...].astype(F32)
            for q in range(quarters):
                table[side * half : (side + 1) * half, q * LANES : (q + 1) * LANES] = spread_rows[
                    pl.ds(q, half, stride=quarters), :
                ].astype(BF16)

    column = columns_of(places_ref, block * chunks, chunks)
    sent = dot(pick_rows(column, 2 * half), table[...]).astype(BF16)
    hidden = silu(before_ref[...] + dot(sent, w_mid_ref[...])).astype(BF16)
    change = normed(dot(hidden, w_out_ref[...]), gain_ref[...], shift_ref[...])
    old = edges_ref[...]
    live = lax.broadcasted_iota(jnp.int32, (slots, 1), 0) < counts_ref[block]
    new = jnp.where(live, old.astype(F32) + change, old.astype(F32)).astype(BF16)
    new_edges_ref[...] = new
    row = rows_of(places_ref, block * chunks, chunks)
    target = lax.broadcasted_iota(jnp.int32, (2 * half, slots), 0)
    term = dot((row == target).astype(F32).astype(BF16), new)

    @pl.when(block == 0)
    def _():
        total[...] = term

    @pl.when(block > 0)
    def _():
        total[...] += term

    @pl.when(block == pl.num_programs(0) - 1)
    def _():
        for side, ref in enumerate((to_mine_ref, to_other_ref)):
            for q in range(quarters):
                spread_rows[pl.ds(q, half, stride=quarters), :] = total[
                    side * half : (side + 1) * half, q * LANES : (q + 1) * LANES
                ]
            ref[...] = spread_rows[...].astype(BF16)


def node_kernel(
    counts_ref,
    receivers_ref,
    new_edges_ref,
    nodes_ref,
    w_in_ref,
    w_out_ref,
    gain_ref,
    shift_ref,
    out_ref,
):
    blocks = counts_ref.shape[0]
    slots = new_edges_ref.shape[0] // blocks
    node_rows, latent = nodes_ref.shape
    block_size = node_rows // blocks
    chunks = slots // LANES
    sums = []
    for b in range(blocks):
        row = rows_of(receivers_ref, b * chunks, chunks)
        slot = lax.broadcasted_iota(jnp.int32, (1, slots), 1)
        row = jnp.where(slot < counts_ref[b], row, -1)
        target = lax.broadcasted_iota(jnp.int32, (block_size, slots), 0)
        pick = (row == target).astype(F32).astype(BF16)
        sums.append(dot(pick, new_edges_ref[b * slots : (b + 1) * slots, :]).astype(BF16))
    fine_sum = jnp.concatenate(sums, axis=0)
    nodes = nodes_ref[...]
    hidden = silu(dot(nodes, w_in_ref[:latent, :]) + dot(fine_sum, w_in_ref[latent:, :]))
    change = normed(dot(hidden.astype(BF16), w_out_ref[...]), gain_ref[...], shift_ref[...])
    out_ref[...] = (nodes.astype(F32) + change).astype(BF16)


def coarse_kernel(
    parts_ref,
    coarse_ref,
    w_in_ref,
    w_out_ref,
    gain_ref,
    shift_ref,
    out_ref,
    rows,
    joined,
):
    owned, latent = coarse_ref.shape
    quarters = latent // LANES
    rows[...] = jnp.sum(parts_ref[...].astype(F32), axis=0)
    joined[...] = jnp.zeros(joined.shape, F32)
    coarse = coarse_ref[...].astype(F32)
    joined[:owned, :latent] = coarse
    for q in range(quarters):
        joined[:owned, latent + q * LANES : latent + (q + 1) * LANES] = rows[
            pl.ds(q, owned, stride=quarters), :
        ]
    hidden = silu(dot(joined[...].astype(BF16), w_in_ref[...])).astype(BF16)
    change = normed(dot(hidden, w_out_ref[...]), gain_ref[...], shift_ref[...])
    out_ref[...] = (coarse + change[:owned, :]).astype(BF16)


def whole(shape):
    return pl.BlockSpec(shape, lambda *_: (0,) * len(shape))


def on_device(
    nodes,
    coarse,
    edges,
    senders,
    receivers,
    counts,
    edge_in,
    edge_out,
    edge_gain,
    edge_shift,
    node_in,
    node_out,
    node_gain,
    node_shift,
):
    node_rows, latent = nodes.shape
    owned = coarse.shape[0]
    blocks = counts.shape[0]
    slot_count = edges.shape[0]
    slots = slot_count // blocks
    regions = lax.axis_size("region")
    peers = regions * lax.axis_size("pair")
    core = lax.axis_index("core")
    smem = pl.BlockSpec(memory_space=pltpu.SMEM)
    params = pltpu.CompilerParams(vmem_limit_bytes=VMEM_LIMIT)
    gain_e, shift_e = edge_gain.reshape(1, latent), edge_shift.reshape(1, latent)
    gain_n, shift_n = node_gain.reshape(1, latent), node_shift.reshape(1, latent)
    swap = [(0, 1), (1, 0)]

    small = coarse.reshape(-1, LANES)
    copies = jnp.broadcast_to(small[None], (peers,) + small.shape)
    table_mine = lax.all_to_all(copies, ("region", "pair"), 0, 0, tiled=True)
    table_mine = table_mine.reshape(-1, LANES)
    table_other = lax.ppermute(table_mine, "core", swap)

    forward = [(i, i + 1) for i in range(regions - 1)]
    backward = [(i + 1, i) for i in range(regions - 1)]
    low = lax.ppermute(nodes, "region", forward)
    high = lax.ppermute(nodes, "region", backward)

    send_grid = senders.reshape(-1, LANES)
    recv_grid = receivers.reshape(-1, LANES)
    slot_ids = jnp.arange(slot_count, dtype=jnp.int32)
    live = slot_ids % slots < jnp.repeat(counts, slots)
    ident = senders - 3 * node_rows
    side = ((ident // owned) % 2) ^ core
    place = side * (peers * owned) + (ident // (2 * owned)) * owned + ident % owned
    places = jnp.where(live & (ident >= 0), place, -1).reshape(-1, LANES)

    row_block = pl.BlockSpec((slots, latent), lambda b: (b, 0))
    before = pl.pallas_call(
        gather_kernel,
        grid=(blocks,),
        in_specs=[
            whole(send_grid.shape),
            whole(recv_grid.shape),
            row_block,
            whole(nodes.shape),
            whole(nodes.shape),
            whole(nodes.shape),
            whole(edge_in.shape),
        ],
        out_specs=row_block,
        out_shape=jax.ShapeDtypeStruct((slot_count, latent), F32),
        compiler_params=params,
        cost_estimate=pl.CostEstimate(
            flops=2 * slot_count * latent * (3 * latent + 3 * node_rows + LANES),
            bytes_accessed=8 * 1024 * 1024,
            transcendentals=0,
        ),
        name="gather",
    )(send_grid, recv_grid, edges, low, nodes, high, edge_in)

    half = peers * owned
    flat = jax.ShapeDtypeStruct(table_mine.shape, BF16)
    new_edges, to_mine, to_other = pl.pallas_call(
        edge_kernel,
        grid=(blocks,),
        in_specs=[
            smem,
            whole(places.shape),
            row_block,
            row_block,
            whole(table_mine.shape),
            whole(table_mine.shape),
            pl.BlockSpec((latent, latent), lambda b: (1, 0)),
            whole(edge_out.shape),
            whole(gain_e.shape),
            whole(gain_e.shape),
        ],
        out_specs=[row_block, whole(flat.shape), whole(flat.shape)],
        out_shape=[jax.ShapeDtypeStruct(edges.shape, BF16), flat, flat],
        scratch_shapes=[
            pltpu.VMEM((2 * half, latent), BF16),
            pltpu.VMEM(flat.shape, F32),
            pltpu.VMEM((2 * half, latent), F32),
        ],
        compiler_params=params,
        cost_estimate=pl.CostEstimate(
            flops=8 * slot_count * latent * latent,
            bytes_accessed=8 * 1024 * 1024,
            transcendentals=slot_count * latent,
        ),
        name="edges",
    )(
        counts,
        places,
        before,
        edges,
        table_mine,
        table_other,
        edge_in,
        edge_out,
        gain_e,
        shift_e,
    )

    arrived = lax.ppermute(to_other, "core", swap)
    chip_sum = (to_mine.astype(F32) + arrived.astype(F32)).astype(BF16)
    parts = lax.all_to_all(
        chip_sum.reshape((peers,) + small.shape), ("region", "pair"), 0, 0, tiled=True
    )

    new_nodes = pl.pallas_call(
        node_kernel,
        in_specs=[smem] + [pl.BlockSpec(memory_space=pltpu.VMEM)] * 7,
        out_specs=pl.BlockSpec(memory_space=pltpu.VMEM),
        out_shape=jax.ShapeDtypeStruct(nodes.shape, BF16),
        compiler_params=params,
        cost_estimate=pl.CostEstimate(
            flops=2 * node_rows * latent * (3 * latent + slots),
            bytes_accessed=4 * 1024 * 1024,
            transcendentals=node_rows * latent,
        ),
        name="fine_nodes",
    )(counts, recv_grid, new_edges, nodes, node_in, node_out, gain_n, shift_n)

    new_coarse = pl.pallas_call(
        coarse_kernel,
        in_specs=[pl.BlockSpec(memory_space=pltpu.VMEM)] * 6,
        out_specs=pl.BlockSpec(memory_space=pltpu.VMEM),
        out_shape=jax.ShapeDtypeStruct(coarse.shape, BF16),
        scratch_shapes=[pltpu.VMEM(small.shape, F32), pltpu.VMEM((8, 2 * latent), F32)],
        compiler_params=params,
        name="coarse_nodes",
    )(parts, coarse, node_in, node_out, gain_n, shift_n)
    return (new_nodes, new_coarse, new_edges)


def solution(mesh):
    regions, groups = mesh.devices.shape
    fine = Mesh(mesh.devices.reshape(regions, groups // 2, 2), ("region", "pair", "core"))
    every = ("region", "pair", "core")
    rows, flat, copied = P(every, None), P(every), P()
    return jax.shard_map(
        on_device,
        mesh=fine,
        in_specs=(rows, rows, rows, flat, flat, flat) + (copied,) * 8,
        out_specs=(rows, rows, rows),
        check_vma=False,
    )
```

```python
import jax
import jax.numpy as jnp
from jax import lax
from jax.experimental import pallas as pl
from jax.experimental.pallas import tpu as pltpu
from jax.sharding import Mesh, PartitionSpec as P

F32 = jnp.float32
BF16 = jnp.bfloat16
LANES = 128
OWNED = 2
STEP = 6
MIB = 1024 * 1024


def dot(a, b):
    return jnp.dot(a, b, preferred_element_type=F32)


def silu(x):
    half = 0.5 * x
    return half + half * jnp.tanh(half)


def normed(output, gain, shift):
    center = output - jnp.mean(output, axis=-1, keepdims=True)
    spread = jnp.mean(center * center, axis=-1, keepdims=True)
    return center * lax.rsqrt(spread + 1e-05) * gain + shift


def columns_of(ids_ref, first, count):
    parts = []
    for k in range(count):
        row = ids_ref[pl.ds(first + k, 1), :].astype(F32)
        parts.append(jnp.broadcast_to(row, (LANES, LANES)).T)
    return jnp.concatenate(parts, axis=0)


def rows_of(ids_ref, first, count):
    return jnp.concatenate([ids_ref[pl.ds(first + k, 1), :] for k in range(count)], axis=1)


def pick_rows(column, width, offset=0):
    lane = lax.broadcasted_iota(jnp.int32, column.shape, 1).astype(F32)
    parts = [
        (column == lane + float(offset + k * LANES)).astype(F32).astype(BF16)
        for k in range(width // LANES)
    ]
    return jnp.concatenate(parts, axis=1)


def copies_kernel(coarse_ref, out_ref, rows):
    owned, latent = coarse_ref.shape
    coarse = coarse_ref[...].astype(F32)
    for q in range(latent // LANES):
        rows[q * owned : (q + 1) * owned, :] = coarse[:, q * LANES : (q + 1) * LANES]
    out_ref[...] = jnp.broadcast_to(rows[...].astype(BF16)[None], out_ref.shape)


def local_kernel(receivers_ref, edges_ref, nodes_ref, w_edge_ref, w_recv_ref, out_ref):
    block = pl.program_id(0)
    slots = edges_ref.shape[0]
    chunks = slots // LANES
    recv = columns_of(receivers_ref, block * chunks, chunks)
    received = dot(pick_rows(recv, nodes_ref.shape[0]), nodes_ref[...]).astype(BF16)
    out_ref[...] = dot(edges_ref[...], w_edge_ref[...]) + dot(received, w_recv_ref[...])


def edge_update(before, sent, edges, w_mid_ref, w_out_ref, gain_ref, shift_ref):
    hidden = silu(before + dot(sent, w_mid_ref[...])).astype(BF16)
    change = normed(dot(hidden, w_out_ref[...]), gain_ref[...], shift_ref[...])
    return (edges.astype(F32) + change).astype(BF16)


def coarse_edge_kernel(
    places_ref,
    before_ref,
    edges_ref,
    mine_ref,
    other_ref,
    w_in_ref,
    w_out_ref,
    gain_ref,
    shift_ref,
    updated_ref,
    to_mine_ref,
    to_other_ref,
    before,
    edges,
    arrived,
    w_mid,
    w_out,
    table,
    spread_rows,
    updated,
    sent,
    sems,
):
    slot_count, latent = edges.shape
    chunks = slot_count // LANES
    half = table.shape[0] // 2
    peers = half // OWNED
    tiles = chunks // STEP
    tile = STEP * LANES

    def copy(src, dst, k):
        one = pltpu.make_async_copy(src, dst, sems.at[k])
        one.start()
        return one

    sides = [copy(ref, arrived.at[i], i) for i, ref in enumerate((mine_ref, other_ref))]
    for side in sides:
        side.wait()
    weights = copy(w_in_ref.at[pl.ds(latent, latent), :], w_mid, 2)
    inputs = []
    for t in range(tiles):
        rows = pl.ds(t * tile, tile)
        inputs.append(
            [
                copy(before_ref.at[rows, :], before.at[rows, :], 4 + 3 * t),
                copy(edges_ref.at[rows, :], edges.at[rows, :], 5 + 3 * t),
            ]
        )
        if t == 0:
            weights_out = copy(w_out_ref, w_out, 3)
    for i in range(2):
        spread_rows[...] = arrived[i].astype(F32)
        for r in range(8):
            q, j = r // OWNED, r % OWNED
            first = i * half + j * peers
            table[first : first + peers, q * LANES : (q + 1) * LANES] = spread_rows[
                pl.ds(r, peers, stride=8), :
            ].astype(BF16)
    for t in range(tiles):
        rows = slice(t * tile, (t + 1) * tile)
        column = columns_of(places_ref, t * STEP, STEP)
        sent[rows, :] = dot(pick_rows(column, 2 * half), table[...]).astype(BF16)
    weights.wait()
    results = []
    for t in range(tiles):
        for one in inputs[t]:
            one.wait()
        if t == 0:
            weights_out.wait()
        rows = slice(t * tile, (t + 1) * tile)
        updated[rows, :] = edge_update(
            before[rows, :], sent[rows, :], edges[rows, :], w_mid, w_out, gain_ref, shift_ref
        )
        results.append(
            copy(
                updated.at[pl.ds(t * tile, tile), :],
                updated_ref.at[pl.ds(t * tile, tile), :],
                6 + 3 * t,
            )
        )
    row = rows_of(places_ref, 0, chunks)
    target = lax.broadcasted_iota(jnp.int32, (half, slot_count), 0)
    for i, ref in enumerate((to_mine_ref, to_other_ref)):
        pick = (row == target + i * half).astype(F32).astype(BF16)
        total = dot(pick, updated[...])
        for r in range(8):
            q, j = r // OWNED, r % OWNED
            spread_rows[pl.ds(r, peers, stride=8), :] = total[
                j * peers : (j + 1) * peers, q * LANES : (q + 1) * LANES
            ]
        ref[...] = spread_rows[...].astype(BF16)
    for one in results:
        one.wait()


def fine_edge_kernel(
    counts_ref,
    senders_ref,
    receivers_ref,
    before_ref,
    edges_ref,
    updated_ref,
    low_ref,
    nodes_ref,
    high_ref,
    w_mid_ref,
    w_out_ref,
    gain_ref,
    shift_ref,
    node_in_ref,
    node_out_ref,
    node_gain_ref,
    node_shift_ref,
    new_edges_ref,
    new_nodes_ref,
):
    block = pl.program_id(0)
    slots, latent = edges_ref.shape
    node_rows = nodes_ref.shape[0]
    block_size = new_nodes_ref.shape[0]
    chunks = slots // LANES
    fresh = []
    for k in range(0, chunks, STEP):
        rows = slice(k * LANES, (k + STEP) * LANES)
        column = columns_of(senders_ref, block * chunks + k, STEP)
        sent = (
            dot(pick_rows(column, node_rows), low_ref[...])
            + dot(pick_rows(column, node_rows, node_rows), nodes_ref[...])
            + dot(pick_rows(column, node_rows, 2 * node_rows), high_ref[...])
        ).astype(BF16)
        old = edges_ref[rows, :]
        new = edge_update(
            before_ref[rows, :], sent, old, w_mid_ref, w_out_ref, gain_ref, shift_ref
        )
        new = jnp.where(column[:, :1] < float(3 * node_rows), new, updated_ref[rows, :])
        slot = lax.broadcasted_iota(jnp.int32, (STEP * LANES, 1), 0) + k * LANES
        new = jnp.where(slot < counts_ref[block], new, old)
        new_edges_ref[rows, :] = new
        fresh.append(new)
    row = rows_of(receivers_ref, block * chunks, chunks)
    slot = lax.broadcasted_iota(jnp.int32, (1, slots), 1)
    row = jnp.where(slot < counts_ref[block], row, -1)
    target = lax.broadcasted_iota(jnp.int32, (block_size, slots), 0)
    pick = (row == target).astype(F32).astype(BF16)
    fine_sum = dot(pick, jnp.concatenate(fresh, axis=0)).astype(BF16)
    nodes = nodes_ref[pl.ds(pl.multiple_of(block * block_size, block_size), block_size), :]
    hidden = silu(dot(nodes, node_in_ref[:latent, :]) + dot(fine_sum, node_in_ref[latent:, :]))
    change = normed(
        dot(hidden.astype(BF16), node_out_ref[...]), node_gain_ref[...], node_shift_ref[...]
    )
    new_nodes_ref[...] = (nodes.astype(F32) + change).astype(BF16)


def coarse_kernel(
    parts_ref,
    coarse_ref,
    w_in_ref,
    w_out_ref,
    gain_ref,
    shift_ref,
    out_ref,
    rows,
    joined,
):
    owned, latent = coarse_ref.shape
    quarters = latent // LANES
    rows[...] = jnp.sum(parts_ref[...].astype(F32), axis=0)
    joined[...] = jnp.zeros(joined.shape, F32)
    coarse = coarse_ref[...].astype(F32)
    joined[:owned, :latent] = coarse
    for q in range(quarters):
        joined[:owned, latent + q * LANES : latent + (q + 1) * LANES] = rows[
            q * owned : (q + 1) * owned, :
        ]
    hidden = silu(dot(joined[...].astype(BF16), w_in_ref[...])).astype(BF16)
    change = normed(dot(hidden, w_out_ref[...]), gain_ref[...], shift_ref[...])
    out_ref[...] = (coarse + change[:owned, :]).astype(BF16)


def whole(shape):
    return pl.BlockSpec(shape, lambda *_: (0,) * len(shape))


def in_hbm(*arrays):
    return [pltpu.with_memory_space_constraint(a, pltpu.HBM) for a in arrays]


def coarse_edges(
    places, before, edges, table_mine, table_other, edge_in, edge_out, gain, shift
):
    slot_count, latent = edges.shape
    flat = jax.ShapeDtypeStruct(table_mine.shape, BF16)
    half = flat.shape[0] * flat.shape[1] // latent
    tiles = slot_count // (STEP * LANES)
    vmem, anywhere = pl.BlockSpec(memory_space=pltpu.VMEM), pl.BlockSpec(memory_space=pl.ANY)
    before, edges, edge_in, edge_out = in_hbm(before, edges, edge_in, edge_out)
    return pl.pallas_call(
        coarse_edge_kernel,
        in_specs=[vmem] + [anywhere] * 6 + [vmem] * 2,
        out_specs=[anywhere, vmem, vmem],
        out_shape=[pltpu.HBM(edges.shape, BF16), flat, flat],
        scratch_shapes=[
            pltpu.VMEM(before.shape, F32),
            pltpu.VMEM(edges.shape, BF16),
            pltpu.VMEM((2,) + flat.shape, BF16),
            pltpu.VMEM((latent, latent), BF16),
            pltpu.VMEM((latent, latent), BF16),
            pltpu.VMEM((2 * half, latent), BF16),
            pltpu.VMEM(flat.shape, F32),
            pltpu.VMEM(edges.shape, BF16),
            pltpu.VMEM(edges.shape, BF16),
            pltpu.SemaphoreType.DMA((4 + 3 * tiles,)),
        ],
        compiler_params=pltpu.CompilerParams(vmem_limit_bytes=40 * MIB),
        cost_estimate=pl.CostEstimate(flops=0, bytes_accessed=0, transcendentals=0),
        name="coarse_edges",
    )(places, before, edges, table_mine, table_other, edge_in, edge_out, gain, shift)


def on_device(
    nodes,
    coarse,
    edges,
    senders,
    receivers,
    counts,
    edge_in,
    edge_out,
    edge_gain,
    edge_shift,
    node_in,
    node_out,
    node_gain,
    node_shift,
):
    node_rows, latent = nodes.shape
    owned = coarse.shape[0]
    blocks = counts.shape[0]
    slot_count = edges.shape[0]
    slots = slot_count // blocks
    regions = lax.axis_size("region")
    peers = regions * lax.axis_size("pair")
    core = lax.axis_index("core")
    smem = pl.BlockSpec(memory_space=pltpu.SMEM)
    gain_e, shift_e = edge_gain.reshape(1, latent), edge_shift.reshape(1, latent)
    gain_n, shift_n = node_gain.reshape(1, latent), node_shift.reshape(1, latent)
    swap = [(0, 1), (1, 0)]

    chunk = (owned * latent // LANES, LANES)
    copies = pl.pallas_call(
        copies_kernel,
        in_specs=[pl.BlockSpec(memory_space=pltpu.VMEM)],
        out_specs=pl.BlockSpec(memory_space=pltpu.VMEM),
        out_shape=jax.ShapeDtypeStruct((peers,) + chunk, BF16),
        scratch_shapes=[pltpu.VMEM(chunk, F32)],
        name="copies",
    )(coarse)
    table_mine = lax.all_to_all(copies, ("region", "pair"), 0, 0, tiled=True)
    table_mine = table_mine.reshape(-1, LANES)
    forward = [(i, i + 1) for i in range(regions - 1)]
    backward = [(i + 1, i) for i in range(regions - 1)]
    low = lax.ppermute(nodes, "region", forward)
    high = lax.ppermute(nodes, "region", backward)

    send_grid = senders.reshape(-1, LANES)
    recv_grid = receivers.reshape(-1, LANES)
    slot_ids = jnp.arange(slot_count, dtype=jnp.int32)
    live = slot_ids % slots < jnp.repeat(counts, slots)
    ident = senders - 3 * node_rows
    side = ((ident // owned) % 2) ^ core
    place = (side * owned + ident % owned) * peers + ident // (2 * owned)
    places = jnp.where(live & (ident >= 0), place, -1).reshape(-1, LANES)

    row_block = pl.BlockSpec((slots, latent), lambda b: (b, 0))
    node_block = pl.BlockSpec((node_rows // blocks, latent), lambda b: (b, 0))

    def w_part(k):
        return pl.BlockSpec((latent, latent), lambda b: (k, 0))

    before = pl.pallas_call(
        local_kernel,
        grid=(blocks,),
        in_specs=[whole(recv_grid.shape), row_block, node_block, w_part(0), w_part(2)],
        out_specs=row_block,
        out_shape=jax.ShapeDtypeStruct((slot_count, latent), F32),
        compiler_params=pltpu.CompilerParams(vmem_limit_bytes=60 * MIB),
        cost_estimate=pl.CostEstimate(
            flops=2 * slot_count * latent * (2 * latent + LANES),
            bytes_accessed=6 * MIB,
            transcendentals=0,
        ),
        name="local",
    )(*in_hbm(recv_grid, edges, nodes, edge_in, edge_in))

    table_mine, before, places = lax.optimization_barrier((table_mine, before, places))
    table_other = lax.ppermute(table_mine, "core", swap)

    before, low, high = lax.optimization_barrier((before, low, high))
    updated, to_mine, to_other = coarse_edges(
        places, before, edges, table_mine, table_other, edge_in, edge_out, gain_e, shift_e
    )
    arrived = lax.ppermute(to_other, "core", swap)
    chip_sum = (to_mine.astype(F32) + arrived.astype(F32)).astype(BF16)
    chip_sum, updated = lax.optimization_barrier((chip_sum, updated))
    parts = lax.all_to_all(
        chip_sum.reshape((peers,) + chunk), ("region", "pair"), 0, 0, tiled=True
    )

    new_edges, new_nodes = pl.pallas_call(
        fine_edge_kernel,
        grid=(blocks,),
        in_specs=[
            smem,
            whole(send_grid.shape),
            whole(recv_grid.shape),
            row_block,
            row_block,
            row_block,
            whole(nodes.shape),
            whole(nodes.shape),
            whole(nodes.shape),
            w_part(1),
            whole(edge_out.shape),
            whole(gain_e.shape),
            whole(gain_e.shape),
            whole(node_in.shape),
            whole(node_out.shape),
            whole(gain_n.shape),
            whole(gain_n.shape),
        ],
        out_specs=[row_block, node_block],
        out_shape=[
            jax.ShapeDtypeStruct(edges.shape, BF16),
            jax.ShapeDtypeStruct(nodes.shape, BF16),
        ],
        compiler_params=pltpu.CompilerParams(vmem_limit_bytes=60 * MIB),
        cost_estimate=pl.CostEstimate(
            flops=2 * slot_count * latent * (4 * latent + 2 * LANES),
            bytes_accessed=10 * MIB,
            transcendentals=slot_count * latent,
        ),
        name="fine_edges",
    )(
        counts,
        send_grid,
        recv_grid,
        before,
        edges,
        updated,
        low,
        nodes,
        high,
        edge_in,
        edge_out,
        gain_e,
        shift_e,
        node_in,
        node_out,
        gain_n,
        shift_n,
    )

    new_coarse = pl.pallas_call(
        coarse_kernel,
        in_specs=[pl.BlockSpec(memory_space=pltpu.VMEM)] * 6,
        out_specs=pl.BlockSpec(memory_space=pltpu.VMEM),
        out_shape=jax.ShapeDtypeStruct(coarse.shape, BF16),
        scratch_shapes=[pltpu.VMEM(chunk, F32), pltpu.VMEM((8, 2 * latent), F32)],
        compiler_params=pltpu.CompilerParams(vmem_limit_bytes=16 * MIB),
        name="coarse_nodes",
    )(parts, coarse, node_in, node_out, gain_n, shift_n)
    return (new_nodes, new_coarse, new_edges)


def solution(mesh):
    regions, groups = mesh.devices.shape
    fine = Mesh(mesh.devices.reshape(regions, groups // 2, 2), ("region", "pair", "core"))
    every = ("region", "pair", "core")
    rows, flat, copied = P(every, None), P(every), P()
    return jax.shard_map(
        on_device,
        mesh=fine,
        in_specs=(rows, rows, rows, flat, flat, flat) + (copied,) * 8,
        out_specs=(rows, rows, rows),
        check_vma=False,
    )
```

```python
import functools

import jax
import jax.numpy as jnp
from jax import lax
from jax.experimental import pallas as pl
from jax.experimental.pallas import tpu as pltpu
from jax.sharding import Mesh, PartitionSpec as P

F32 = jnp.float32
BF16 = jnp.bfloat16
LANES = 128
OWNED = 2
STEP = 6
MIB = 1024 * 1024


def dot(a, b):
    return jnp.dot(a, b, preferred_element_type=F32)


def silu(x):
    half = 0.5 * x
    return half + half * jnp.tanh(half)


def normed(output, gain, shift):
    center = output - jnp.mean(output, axis=-1, keepdims=True)
    spread = jnp.mean(center * center, axis=-1, keepdims=True)
    return center * lax.rsqrt(spread + 1e-05) * gain + shift


def columns_of(ids_ref, first, count):
    parts = []
    for k in range(count):
        row = ids_ref[pl.ds(first + k, 1), :].astype(F32)
        parts.append(jnp.broadcast_to(row, (LANES, LANES)).T)
    return jnp.concatenate(parts, axis=0)


def rows_of(ids_ref, first, count):
    return jnp.concatenate([ids_ref[pl.ds(first + k, 1), :] for k in range(count)], axis=1)


def pick_rows(column, width, offset=0):
    lane = lax.broadcasted_iota(jnp.int32, column.shape, 1).astype(F32)
    parts = [
        (column == lane + float(offset + k * LANES)).astype(F32).astype(BF16)
        for k in range(width // LANES)
    ]
    return jnp.concatenate(parts, axis=1)


def copies_kernel(coarse_ref, out_ref, rows):
    owned, latent = coarse_ref.shape
    coarse = coarse_ref[...].astype(F32)
    for q in range(latent // LANES):
        rows[q * owned : (q + 1) * owned, :] = coarse[:, q * LANES : (q + 1) * LANES]
    out_ref[...] = jnp.broadcast_to(rows[...].astype(BF16)[None], out_ref.shape)


def local_kernel(receivers_ref, edges_ref, nodes_ref, w_edge_ref, w_recv_ref, out_ref):
    block = pl.program_id(0)
    slots = edges_ref.shape[0]
    chunks = slots // LANES
    recv = columns_of(receivers_ref, block * chunks, chunks)
    received = dot(pick_rows(recv, nodes_ref.shape[0]), nodes_ref[...]).astype(BF16)
    out_ref[...] = dot(edges_ref[...], w_edge_ref[...]) + dot(received, w_recv_ref[...])


def edge_update(before, sent, edges, w_mid_ref, w_out_ref, gain_ref, shift_ref):
    hidden = silu(before + dot(sent, w_mid_ref[...])).astype(BF16)
    change = normed(dot(hidden, w_out_ref[...]), gain_ref[...], shift_ref[...])
    return (edges.astype(F32) + change).astype(BF16)


def coarse_edge_kernel(
    core_ref,
    places_ref,
    before_ref,
    edges_ref,
    table_ref,
    w_in_ref,
    w_out_ref,
    gain_ref,
    shift_ref,
    updated_ref,
    to_mine_ref,
    to_other_ref,
    before,
    edges,
    arrived,
    w_mid,
    w_out,
    table,
    spread_rows,
    updated,
    sent,
    sems,
):
    slot_count, latent = edges.shape
    chunks = slot_count // LANES
    half = table.shape[0] // 2
    peers = half // OWNED
    tiles = chunks // STEP
    tile = STEP * LANES

    def copy(src, dst, k):
        one = pltpu.make_async_copy(src, dst, sems.at[k])
        one.start()
        return one

    copy(table_ref, arrived, 0).wait()
    weights = copy(w_in_ref.at[pl.ds(latent, latent), :], w_mid, 2)
    inputs = []
    for t in range(tiles):
        rows = pl.ds(t * tile, tile)
        inputs.append(
            [
                copy(before_ref.at[rows, :], before.at[rows, :], 4 + 3 * t),
                copy(edges_ref.at[rows, :], edges.at[rows, :], 5 + 3 * t),
            ]
        )
        if t == 0:
            weights_out = copy(w_out_ref, w_out, 3)
    spread_rows[...] = arrived[...].astype(F32)

    def fill_table(core):
        for side in range(2):
            for r in range(8):
                q, j = r // OWNED, r % OWNED
                first = side * half + j * peers
                table[first : first + peers, q * LANES : (q + 1) * LANES] = spread_rows[
                    pl.ds(8 * (side ^ core) + r, peers, stride=16), :
                ].astype(BF16)

    for core in range(2):
        pl.when(core_ref[0] == core)(functools.partial(fill_table, core))
    for t in range(tiles):
        rows = slice(t * tile, (t + 1) * tile)
        column = columns_of(places_ref, t * STEP, STEP)
        sent[rows, :] = dot(pick_rows(column, 2 * half), table[...]).astype(BF16)
    weights.wait()
    results = []
    for t in range(tiles):
        for one in inputs[t]:
            one.wait()
        if t == 0:
            weights_out.wait()
        rows = slice(t * tile, (t + 1) * tile)
        updated[rows, :] = edge_update(
            before[rows, :], sent[rows, :], edges[rows, :], w_mid, w_out, gain_ref, shift_ref
        )
        results.append(
            copy(
                updated.at[pl.ds(t * tile, tile), :],
                updated_ref.at[pl.ds(t * tile, tile), :],
                6 + 3 * t,
            )
        )
    row = rows_of(places_ref, 0, chunks)
    target = lax.broadcasted_iota(jnp.int32, (2 * half, slot_count), 0)
    total = dot((row == target).astype(F32).astype(BF16), updated[...])
    for i, ref in enumerate((to_mine_ref, to_other_ref)):
        for r in range(8):
            q, j = r // OWNED, r % OWNED
            first = i * half + j * peers
            spread_rows[pl.ds(r, peers, stride=8), :] = total[
                first : first + peers, q * LANES : (q + 1) * LANES
            ]
        ref[...] = spread_rows[: half * latent // LANES, :].astype(BF16)
    for one in results:
        one.wait()


def fine_edge_kernel(
    counts_ref,
    senders_ref,
    receivers_ref,
    before_ref,
    edges_ref,
    updated_ref,
    low_ref,
    nodes_ref,
    high_ref,
    w_mid_ref,
    w_out_ref,
    gain_ref,
    shift_ref,
    node_in_ref,
    node_out_ref,
    node_gain_ref,
    node_shift_ref,
    new_edges_ref,
    new_nodes_ref,
):
    block = pl.program_id(0)
    slots, latent = edges_ref.shape
    node_rows = nodes_ref.shape[0]
    block_size = new_nodes_ref.shape[0]
    chunks = slots // LANES
    fresh = []
    for k in range(0, chunks, STEP):
        rows = slice(k * LANES, (k + STEP) * LANES)
        column = columns_of(senders_ref, block * chunks + k, STEP)
        sent = (
            dot(pick_rows(column, node_rows), low_ref[...])
            + dot(pick_rows(column, node_rows, node_rows), nodes_ref[...])
            + dot(pick_rows(column, node_rows, 2 * node_rows), high_ref[...])
        ).astype(BF16)
        old = edges_ref[rows, :]
        new = edge_update(
            before_ref[rows, :], sent, old, w_mid_ref, w_out_ref, gain_ref, shift_ref
        )
        new = jnp.where(column[:, :1] < float(3 * node_rows), new, updated_ref[rows, :])
        slot = lax.broadcasted_iota(jnp.int32, (STEP * LANES, 1), 0) + k * LANES
        new = jnp.where(slot < counts_ref[block], new, old)
        new_edges_ref[rows, :] = new
        fresh.append(new)
    row = rows_of(receivers_ref, block * chunks, chunks)
    slot = lax.broadcasted_iota(jnp.int32, (1, slots), 1)
    row = jnp.where(slot < counts_ref[block], row, -1)
    target = lax.broadcasted_iota(jnp.int32, (block_size, slots), 0)
    pick = (row == target).astype(F32).astype(BF16)
    fine_sum = dot(pick, jnp.concatenate(fresh, axis=0)).astype(BF16)
    nodes = nodes_ref[pl.ds(pl.multiple_of(block * block_size, block_size), block_size), :]
    hidden = silu(dot(nodes, node_in_ref[:latent, :]) + dot(fine_sum, node_in_ref[latent:, :]))
    change = normed(
        dot(hidden.astype(BF16), node_out_ref[...]), node_gain_ref[...], node_shift_ref[...]
    )
    new_nodes_ref[...] = (nodes.astype(F32) + change).astype(BF16)


def coarse_kernel(
    parts_ref,
    coarse_ref,
    w_in_ref,
    w_out_ref,
    gain_ref,
    shift_ref,
    out_ref,
    rows,
    joined,
):
    owned, latent = coarse_ref.shape
    quarters = latent // LANES
    rows[...] = jnp.sum(parts_ref[...].astype(F32), axis=0)
    joined[...] = jnp.zeros(joined.shape, F32)
    coarse = coarse_ref[...].astype(F32)
    joined[:owned, :latent] = coarse
    for q in range(quarters):
        joined[:owned, latent + q * LANES : latent + (q + 1) * LANES] = rows[
            q * owned : (q + 1) * owned, :
        ]
    hidden = silu(dot(joined[...].astype(BF16), w_in_ref[...])).astype(BF16)
    change = normed(dot(hidden, w_out_ref[...]), gain_ref[...], shift_ref[...])
    out_ref[...] = (coarse + change[:owned, :]).astype(BF16)


def whole(shape):
    return pl.BlockSpec(shape, lambda *_: (0,) * len(shape))


def in_hbm(*arrays):
    return [pltpu.with_memory_space_constraint(a, pltpu.HBM) for a in arrays]


def coarse_edges(
    core, places, before, edges, table, edge_in, edge_out, gain, shift
):
    slot_count, latent = edges.shape
    flat = jax.ShapeDtypeStruct((table.shape[0] // 2, LANES), BF16)
    half = flat.shape[0] * flat.shape[1] // latent
    tiles = slot_count // (STEP * LANES)
    smem = pl.BlockSpec(memory_space=pltpu.SMEM)
    vmem, anywhere = pl.BlockSpec(memory_space=pltpu.VMEM), pl.BlockSpec(memory_space=pl.ANY)
    before, edges, edge_in, edge_out = in_hbm(before, edges, edge_in, edge_out)
    return pl.pallas_call(
        coarse_edge_kernel,
        in_specs=[smem, vmem] + [anywhere] * 5 + [vmem] * 2,
        out_specs=[anywhere, vmem, vmem],
        out_shape=[pltpu.HBM(edges.shape, BF16), flat, flat],
        scratch_shapes=[
            pltpu.VMEM(before.shape, F32),
            pltpu.VMEM(edges.shape, BF16),
            pltpu.VMEM(table.shape, BF16),
            pltpu.VMEM((latent, latent), BF16),
            pltpu.VMEM((latent, latent), BF16),
            pltpu.VMEM((2 * half, latent), BF16),
            pltpu.VMEM(table.shape, F32),
            pltpu.VMEM(edges.shape, BF16),
            pltpu.VMEM(edges.shape, BF16),
            pltpu.SemaphoreType.DMA((4 + 3 * tiles,)),
        ],
        compiler_params=pltpu.CompilerParams(vmem_limit_bytes=40 * MIB),
        cost_estimate=pl.CostEstimate(flops=0, bytes_accessed=0, transcendentals=0),
        name="coarse_edges",
    )(core, places, before, edges, table, edge_in, edge_out, gain, shift)


def on_device(
    nodes,
    coarse,
    edges,
    senders,
    receivers,
    counts,
    edge_in,
    edge_out,
    edge_gain,
    edge_shift,
    node_in,
    node_out,
    node_gain,
    node_shift,
):
    node_rows, latent = nodes.shape
    owned = coarse.shape[0]
    blocks = counts.shape[0]
    slot_count = edges.shape[0]
    slots = slot_count // blocks
    regions = lax.axis_size("region")
    peers = regions * lax.axis_size("pair")
    core = lax.axis_index("core")
    smem = pl.BlockSpec(memory_space=pltpu.SMEM)
    gain_e, shift_e = edge_gain.reshape(1, latent), edge_shift.reshape(1, latent)
    gain_n, shift_n = node_gain.reshape(1, latent), node_shift.reshape(1, latent)
    swap = [(0, 1), (1, 0)]

    chunk = (owned * latent // LANES, LANES)
    copies = pl.pallas_call(
        copies_kernel,
        in_specs=[pl.BlockSpec(memory_space=pltpu.VMEM)],
        out_specs=pl.BlockSpec(memory_space=pltpu.VMEM),
        out_shape=jax.ShapeDtypeStruct((2 * peers,) + chunk, BF16),
        scratch_shapes=[pltpu.VMEM(chunk, F32)],
        name="copies",
    )(coarse)
    table = lax.all_to_all(copies, ("region", "pair", "core"), 0, 0, tiled=True)
    table = table.reshape(-1, LANES)

    forward = [(i, i + 1) for i in range(regions - 1)]
    backward = [(i + 1, i) for i in range(regions - 1)]
    low = lax.ppermute(nodes, "region", forward)
    high = lax.ppermute(nodes, "region", backward)

    send_grid = senders.reshape(-1, LANES)
    recv_grid = receivers.reshape(-1, LANES)
    slot_ids = jnp.arange(slot_count, dtype=jnp.int32)
    live = slot_ids % slots < jnp.repeat(counts, slots)
    ident = senders - 3 * node_rows
    side = ((ident // owned) % 2) ^ core
    place = (side * owned + ident % owned) * peers + ident // (2 * owned)
    places = jnp.where(live & (ident >= 0), place, -1).reshape(-1, LANES)

    row_block = pl.BlockSpec((slots, latent), lambda b: (b, 0))
    node_block = pl.BlockSpec((node_rows // blocks, latent), lambda b: (b, 0))

    def w_part(k):
        return pl.BlockSpec((latent, latent), lambda b: (k, 0))

    before = pl.pallas_call(
        local_kernel,
        grid=(blocks,),
        in_specs=[whole(recv_grid.shape), row_block, node_block, w_part(0), w_part(2)],
        out_specs=row_block,
        out_shape=jax.ShapeDtypeStruct((slot_count, latent), F32),
        compiler_params=pltpu.CompilerParams(vmem_limit_bytes=60 * MIB),
        cost_estimate=pl.CostEstimate(
            flops=2 * slot_count * latent * (2 * latent + LANES),
            bytes_accessed=6 * MIB,
            transcendentals=0,
        ),
        name="local",
    )(*in_hbm(recv_grid, edges, nodes, edge_in, edge_in))

    table, before, places = lax.optimization_barrier((table, before, places))
    updated, to_mine, to_other = coarse_edges(
        core.reshape(1), places, before, edges, table, edge_in, edge_out, gain_e, shift_e
    )
    to_other, low, high = lax.optimization_barrier((to_other, low, high))
    arrived = lax.ppermute(to_other, "core", swap)
    chip_sum = (to_mine.astype(F32) + arrived.astype(F32)).astype(BF16)
    chip_sum, updated = lax.optimization_barrier((chip_sum, updated))
    parts = lax.all_to_all(
        chip_sum.reshape((peers,) + chunk), ("region", "pair"), 0, 0, tiled=True
    )

    new_edges, new_nodes = pl.pallas_call(
        fine_edge_kernel,
        grid=(blocks,),
        in_specs=[
            smem,
            whole(send_grid.shape),
            whole(recv_grid.shape),
            row_block,
            row_block,
            row_block,
            whole(nodes.shape),
            whole(nodes.shape),
            whole(nodes.shape),
            w_part(1),
            whole(edge_out.shape),
            whole(gain_e.shape),
            whole(gain_e.shape),
            whole(node_in.shape),
            whole(node_out.shape),
            whole(gain_n.shape),
            whole(gain_n.shape),
        ],
        out_specs=[row_block, node_block],
        out_shape=[
            jax.ShapeDtypeStruct(edges.shape, BF16),
            jax.ShapeDtypeStruct(nodes.shape, BF16),
        ],
        compiler_params=pltpu.CompilerParams(vmem_limit_bytes=60 * MIB),
        cost_estimate=pl.CostEstimate(
            flops=2 * slot_count * latent * (4 * latent + 2 * LANES),
            bytes_accessed=10 * MIB,
            transcendentals=slot_count * latent,
        ),
        name="fine_edges",
    )(
        counts,
        send_grid,
        recv_grid,
        before,
        edges,
        updated,
        low,
        nodes,
        high,
        edge_in,
        edge_out,
        gain_e,
        shift_e,
        node_in,
        node_out,
        gain_n,
        shift_n,
    )

    new_coarse = pl.pallas_call(
        coarse_kernel,
        in_specs=[pl.BlockSpec(memory_space=pltpu.VMEM)] * 6,
        out_specs=pl.BlockSpec(memory_space=pltpu.VMEM),
        out_shape=jax.ShapeDtypeStruct(coarse.shape, BF16),
        scratch_shapes=[pltpu.VMEM(chunk, F32), pltpu.VMEM((8, 2 * latent), F32)],
        compiler_params=pltpu.CompilerParams(vmem_limit_bytes=16 * MIB),
        name="coarse_nodes",
    )(parts, coarse, node_in, node_out, gain_n, shift_n)
    return (new_nodes, new_coarse, new_edges)


def solution(mesh):
    regions, groups = mesh.devices.shape
    fine = Mesh(mesh.devices.reshape(regions, groups // 2, 2), ("region", "pair", "core"))
    every = ("region", "pair", "core")
    rows, flat, copied = P(every, None), P(every), P()
    return jax.shard_map(
        on_device,
        mesh=fine,
        in_specs=(rows, rows, rows, flat, flat, flat) + (copied,) * 8,
        out_specs=(rows, rows, rows),
        check_vma=False,
    )
```

```python
import functools

import jax
import jax.numpy as jnp
from jax import lax
from jax.experimental import pallas as pl
from jax.experimental.pallas import tpu as pltpu
from jax.sharding import Mesh, PartitionSpec as P

F32 = jnp.float32
BF16 = jnp.bfloat16
LANES = 128
OWNED = 2
FINE = 768
STEP = 6
MIB = 1024 * 1024


def dot(a, b):
    return jnp.dot(a, b, preferred_element_type=F32)


def silu(x):
    half = 0.5 * x
    return half + half * jnp.tanh(half)


def normed(output, gain, shift):
    center = output - jnp.mean(output, axis=-1, keepdims=True)
    spread = jnp.mean(center * center, axis=-1, keepdims=True)
    return center * lax.rsqrt(spread + 1e-05) * gain + shift


def columns_of(ids_ref, first, count):
    parts = []
    for k in range(count):
        row = ids_ref[pl.ds(first + k, 1), :].astype(F32)
        parts.append(jnp.broadcast_to(row, (LANES, LANES)).T)
    return jnp.concatenate(parts, axis=0)


def rows_of(ids_ref, first, count):
    return jnp.concatenate([ids_ref[pl.ds(first + k, 1), :] for k in range(count)], axis=1)


def pick_rows(column, width, offset=0):
    lane = lax.broadcasted_iota(jnp.int32, column.shape, 1).astype(F32)
    parts = [
        (column == lane + float(offset + k * LANES)).astype(F32).astype(BF16)
        for k in range(width // LANES)
    ]
    return jnp.concatenate(parts, axis=1)


def copies_kernel(coarse_ref, out_ref, rows):
    owned, latent = coarse_ref.shape
    coarse = coarse_ref[...].astype(F32)
    for q in range(latent // LANES):
        rows[q * owned : (q + 1) * owned, :] = coarse[:, q * LANES : (q + 1) * LANES]
    out_ref[...] = jnp.broadcast_to(rows[...].astype(BF16)[None], out_ref.shape)


def local_kernel(
    core_ref,
    counts_ref,
    senders_ref,
    receivers_ref,
    edges_ref,
    nodes_ref,
    w_edge_ref,
    w_recv_ref,
    out_ref,
    places_ref,
    *,
    peers,
):
    block = pl.program_id(0)
    shape = places_ref.shape
    per_block = shape[0] // counts_ref.shape[0] * LANES
    row = lax.broadcasted_iota(jnp.int32, shape, 0)
    slot = row * LANES + lax.broadcasted_iota(jnp.int32, shape, 1)
    end = jnp.zeros(shape, jnp.int32)
    for b in range(counts_ref.shape[0]):
        end = jnp.where(slot >= b * per_block, b * per_block + counts_ref[b], end)
    ident = senders_ref[...] - FINE
    side = ((ident >> 1) & 1) ^ core_ref[0]
    place = (side * OWNED + (ident & 1)) * peers + (ident >> 2)
    places_ref[...] = jnp.where((slot < end) & (ident >= 0), place, -1)

    slots = edges_ref.shape[0]
    chunks = slots // LANES
    recv = columns_of(receivers_ref, block * chunks, chunks)
    offered = dot(nodes_ref[...], w_recv_ref[...]).astype(BF16)
    total = dot(edges_ref[...], w_edge_ref[...])
    total += dot(pick_rows(recv, nodes_ref.shape[0]), offered)
    out_ref[...] = total.astype(BF16)


def edge_update(before, sent, edges, w_mid_ref, w_out_ref, gain_ref, shift_ref):
    hidden = silu(before.astype(F32) + dot(sent, w_mid_ref[...])).astype(BF16)
    change = normed(dot(hidden, w_out_ref[...]), gain_ref[...], shift_ref[...])
    return (edges.astype(F32) + change).astype(BF16)


def coarse_edge_kernel(
    core_ref,
    places,
    before_ref,
    edges_ref,
    table_ref,
    w_in_ref,
    w_out_ref,
    gain_ref,
    shift_ref,
    updated_ref,
    to_mine_ref,
    to_other_ref,
    edges,
    w_mid,
    w_out,
    table,
    spread_rows,
    updated,
    sent,
    sems,
):
    slot_count, latent = edges.shape
    chunks = slot_count // LANES
    half = table.shape[0] // 2
    peers = half // OWNED
    tiles = chunks // STEP
    tile = STEP * LANES

    def copy(src, dst, k):
        one = pltpu.make_async_copy(src, dst, sems.at[k])
        one.start()
        return one

    weights = copy(w_in_ref.at[pl.ds(latent, latent), :], w_mid, 2)
    inputs = []
    for t in range(tiles):
        rows = pl.ds(t * tile, tile)
        inputs.append(
            [
                copy(edges_ref.at[rows, :], edges.at[rows, :], 5 + 3 * t),
            ]
        )
        if t == 0:
            weights_out = copy(w_out_ref, w_out, 3)
    spread_rows[...] = table_ref[...].astype(F32)

    def fill_table(core):
        for side in range(2):
            for r in range(8):
                q, j = r // OWNED, r % OWNED
                first = side * half + j * peers
                table[first : first + peers, q * LANES : (q + 1) * LANES] = spread_rows[
                    pl.ds((side ^ core) * 8 * peers + r, peers, stride=8), :
                ].astype(BF16)

    for core in range(2):
        pl.when(core_ref[0] == core)(functools.partial(fill_table, core))
    for t in range(tiles):
        rows = slice(t * tile, (t + 1) * tile)
        column = columns_of(places, t * STEP, STEP)
        sent[rows, :] = dot(pick_rows(column, 2 * half), table[...]).astype(BF16)
    weights.wait()
    results = []
    for t in range(tiles):
        for one in inputs[t]:
            one.wait()
        if t == 0:
            weights_out.wait()
        rows = slice(t * tile, (t + 1) * tile)
        updated[rows, :] = edge_update(
            before_ref[rows, :], sent[rows, :], edges[rows, :], w_mid, w_out, gain_ref, shift_ref
        )
        results.append(
            copy(
                updated.at[pl.ds(t * tile, tile), :],
                updated_ref.at[pl.ds(t * tile, tile), :],
                6 + 3 * t,
            )
        )
    row = rows_of(places, 0, chunks)
    target = lax.broadcasted_iota(jnp.int32, (2 * half, slot_count), 0)
    total = dot((row == target).astype(F32).astype(BF16), updated[...])
    for i, ref in enumerate((to_mine_ref, to_other_ref)):
        for r in range(8):
            q, j = r // OWNED, r % OWNED
            first = i * half + j * peers
            spread_rows[pl.ds(r, peers, stride=8), :] = total[
                first : first + peers, q * LANES : (q + 1) * LANES
            ]
        ref[...] = spread_rows[: half * latent // LANES, :].astype(BF16)
    for one in results:
        one.wait()


def fine_edge_kernel(
    counts_ref,
    senders_ref,
    receivers_ref,
    before_ref,
    edges_ref,
    updated_ref,
    low_ref,
    nodes_ref,
    high_ref,
    w_mid_ref,
    w_out_ref,
    gain_ref,
    shift_ref,
    node_in_ref,
    node_out_ref,
    node_gain_ref,
    node_shift_ref,
    new_edges_ref,
    new_nodes_ref,
):
    block = pl.program_id(0)
    slots, latent = edges_ref.shape
    node_rows = nodes_ref.shape[0]
    block_size = new_nodes_ref.shape[0]
    chunks = slots // LANES
    fresh = []
    for k in range(0, chunks, STEP):
        rows = slice(k * LANES, (k + STEP) * LANES)
        column = columns_of(senders_ref, block * chunks + k, STEP)
        sent = (
            dot(pick_rows(column, node_rows), low_ref[...])
            + dot(pick_rows(column, node_rows, node_rows), nodes_ref[...])
            + dot(pick_rows(column, node_rows, 2 * node_rows), high_ref[...])
        ).astype(BF16)
        old = edges_ref[rows, :]
        new = edge_update(
            before_ref[rows, :], sent, old, w_mid_ref, w_out_ref, gain_ref, shift_ref
        )
        new = jnp.where(column[:, :1] < float(3 * node_rows), new, updated_ref[rows, :])
        slot = lax.broadcasted_iota(jnp.int32, (STEP * LANES, 1), 0) + k * LANES
        new = jnp.where(slot < counts_ref[block], new, old)
        new_edges_ref[rows, :] = new
        fresh.append(new)
    row = rows_of(receivers_ref, block * chunks, chunks)
    slot = lax.broadcasted_iota(jnp.int32, (1, slots), 1)
    row = jnp.where(slot < counts_ref[block], row, -1)
    target = lax.broadcasted_iota(jnp.int32, (block_size, slots), 0)
    pick = (row == target).astype(F32).astype(BF16)
    fine_sum = dot(pick, jnp.concatenate(fresh, axis=0)).astype(BF16)
    nodes = nodes_ref[pl.ds(pl.multiple_of(block * block_size, block_size), block_size), :]
    hidden = silu(dot(nodes, node_in_ref[:latent, :]) + dot(fine_sum, node_in_ref[latent:, :]))
    change = normed(
        dot(hidden.astype(BF16), node_out_ref[...]), node_gain_ref[...], node_shift_ref[...]
    )
    new_nodes_ref[...] = (nodes.astype(F32) + change).astype(BF16)


def coarse_kernel(
    parts_ref,
    coarse_ref,
    w_in_ref,
    w_out_ref,
    gain_ref,
    shift_ref,
    out_ref,
    rows,
    joined,
):
    owned, latent = coarse_ref.shape
    quarters = latent // LANES
    rows[...] = jnp.sum(parts_ref[...].astype(F32), axis=0)
    joined[...] = jnp.zeros(joined.shape, F32)
    coarse = coarse_ref[...].astype(F32)
    joined[:owned, :latent] = coarse
    for q in range(quarters):
        joined[:owned, latent + q * LANES : latent + (q + 1) * LANES] = rows[
            q * owned : (q + 1) * owned, :
        ]
    hidden = silu(dot(joined[...].astype(BF16), w_in_ref[...])).astype(BF16)
    change = normed(dot(hidden, w_out_ref[...]), gain_ref[...], shift_ref[...])
    out_ref[...] = (coarse + change[:owned, :]).astype(BF16)


def whole(shape):
    return pl.BlockSpec(shape, lambda *_: (0,) * len(shape))


def in_hbm(*arrays):
    return [pltpu.with_memory_space_constraint(a, pltpu.HBM) for a in arrays]


def coarse_edges(
    core, places, before, edges, table, edge_in, edge_out, gain, shift
):
    slot_count, latent = edges.shape
    flat = jax.ShapeDtypeStruct((table.shape[0] // 2, LANES), BF16)
    half = flat.shape[0] * flat.shape[1] // latent
    tiles = slot_count // (STEP * LANES)
    smem = pl.BlockSpec(memory_space=pltpu.SMEM)
    vmem, anywhere = pl.BlockSpec(memory_space=pltpu.VMEM), pl.BlockSpec(memory_space=pl.ANY)
    edges, edge_in, edge_out = in_hbm(edges, edge_in, edge_out)
    return pl.pallas_call(
        coarse_edge_kernel,
        in_specs=[smem, vmem, vmem, anywhere, vmem, anywhere, anywhere, vmem, vmem],
        out_specs=[anywhere, vmem, vmem],
        out_shape=[pltpu.HBM(edges.shape, BF16), flat, flat],
        scratch_shapes=[
            pltpu.VMEM(edges.shape, BF16),
            pltpu.VMEM((latent, latent), BF16),
            pltpu.VMEM((latent, latent), BF16),
            pltpu.VMEM((2 * half, latent), BF16),
            pltpu.VMEM(table.shape, F32),
            pltpu.VMEM(edges.shape, BF16),
            pltpu.VMEM(edges.shape, BF16),
            pltpu.SemaphoreType.DMA((4 + 3 * tiles,)),
        ],
        compiler_params=pltpu.CompilerParams(vmem_limit_bytes=40 * MIB),
        cost_estimate=pl.CostEstimate(flops=0, bytes_accessed=0, transcendentals=0),
        name="coarse_edges",
    )(core, places, before, edges, table, edge_in, edge_out, gain, shift)


def on_device(
    nodes,
    coarse,
    edges,
    senders,
    receivers,
    counts,
    edge_in,
    edge_out,
    edge_gain,
    edge_shift,
    node_in,
    node_out,
    node_gain,
    node_shift,
):
    node_rows, latent = nodes.shape
    owned = coarse.shape[0]
    blocks = counts.shape[0]
    slot_count = edges.shape[0]
    slots = slot_count // blocks
    regions = lax.axis_size("region")
    peers = regions * lax.axis_size("pair")
    core = lax.axis_index("core")
    smem = pl.BlockSpec(memory_space=pltpu.SMEM)
    gain_e, shift_e = edge_gain.reshape(1, latent), edge_shift.reshape(1, latent)
    gain_n, shift_n = node_gain.reshape(1, latent), node_shift.reshape(1, latent)
    swap = [(0, 1), (1, 0)]

    chunk = (owned * latent // LANES, LANES)
    copies = pl.pallas_call(
        copies_kernel,
        in_specs=[pl.BlockSpec(memory_space=pltpu.VMEM)],
        out_specs=pl.BlockSpec(memory_space=pltpu.VMEM),
        out_shape=jax.ShapeDtypeStruct((peers,) + chunk, BF16),
        scratch_shapes=[pltpu.VMEM(chunk, F32)],
        name="copies",
    )(coarse)
    table = lax.all_to_all(copies, ("region", "pair"), 0, 0, tiled=True)

    forward = [(i, i + 1) for i in range(regions - 1)]
    backward = [(i + 1, i) for i in range(regions - 1)]
    low = lax.ppermute(nodes, "region", forward)
    high = lax.ppermute(nodes, "region", backward)

    send_grid = senders.reshape(-1, LANES)
    recv_grid = receivers.reshape(-1, LANES)
    row_block = pl.BlockSpec((slots, latent), lambda b: (b, 0))
    node_block = pl.BlockSpec((node_rows // blocks, latent), lambda b: (b, 0))

    def w_part(k):
        return pl.BlockSpec((latent, latent), lambda b: (k, 0))

    core = core.reshape(1)
    before, places = pl.pallas_call(
        functools.partial(local_kernel, peers=peers),
        grid=(blocks,),
        in_specs=[smem, smem, whole(send_grid.shape), whole(recv_grid.shape), row_block, node_block, w_part(0), w_part(2)],
        out_specs=[row_block, whole(send_grid.shape)],
        out_shape=[
            pltpu.VMEM((slot_count, latent), BF16),
            pltpu.VMEM(send_grid.shape, jnp.int32),
        ],
        compiler_params=pltpu.CompilerParams(vmem_limit_bytes=60 * MIB),
        cost_estimate=pl.CostEstimate(
            flops=2 * slot_count * latent * (2 * latent + LANES),
            bytes_accessed=6 * MIB,
            transcendentals=0,
        ),
        name="local",
    )(core, counts, send_grid, recv_grid, *in_hbm(edges, nodes, edge_in, edge_in))

    table, before = lax.optimization_barrier((table, before))
    table = lax.all_gather(table.reshape(-1, LANES), "core", axis=0, tiled=True)
    updated, to_mine, to_other = coarse_edges(
        core, places, before, edges, table, edge_in, edge_out, gain_e, shift_e
    )
    to_other, low, high = lax.optimization_barrier((to_other, low, high))
    arrived = lax.ppermute(to_other, "core", swap)
    chip_sum = (to_mine.astype(F32) + arrived.astype(F32)).astype(BF16)
    chip_sum, updated = lax.optimization_barrier((chip_sum, updated))
    parts = lax.all_to_all(
        chip_sum.reshape((peers,) + chunk), ("region", "pair"), 0, 0, tiled=True
    )

    new_edges, new_nodes = pl.pallas_call(
        fine_edge_kernel,
        grid=(blocks,),
        in_specs=[
            smem,
            whole(send_grid.shape),
            whole(recv_grid.shape),
            row_block,
            row_block,
            row_block,
            whole(nodes.shape),
            whole(nodes.shape),
            whole(nodes.shape),
            w_part(1),
            whole(edge_out.shape),
            whole(gain_e.shape),
            whole(gain_e.shape),
            whole(node_in.shape),
            whole(node_out.shape),
            whole(gain_n.shape),
            whole(gain_n.shape),
        ],
        out_specs=[row_block, node_block],
        out_shape=[
            jax.ShapeDtypeStruct(edges.shape, BF16),
            jax.ShapeDtypeStruct(nodes.shape, BF16),
        ],
        compiler_params=pltpu.CompilerParams(vmem_limit_bytes=60 * MIB),
        cost_estimate=pl.CostEstimate(
            flops=2 * slot_count * latent * (4 * latent + 2 * LANES),
            bytes_accessed=10 * MIB,
            transcendentals=slot_count * latent,
        ),
        name="fine_edges",
    )(
        counts,
        send_grid,
        recv_grid,
        before,
        edges,
        updated,
        low,
        nodes,
        high,
        edge_in,
        edge_out,
        gain_e,
        shift_e,
        node_in,
        node_out,
        gain_n,
        shift_n,
    )

    new_coarse = pl.pallas_call(
        coarse_kernel,
        in_specs=[pl.BlockSpec(memory_space=pltpu.VMEM)] * 6,
        out_specs=pl.BlockSpec(memory_space=pltpu.VMEM),
        out_shape=jax.ShapeDtypeStruct(coarse.shape, BF16),
        scratch_shapes=[pltpu.VMEM(chunk, F32), pltpu.VMEM((8, 2 * latent), F32)],
        compiler_params=pltpu.CompilerParams(vmem_limit_bytes=16 * MIB),
        name="coarse_nodes",
    )(parts, coarse, node_in, node_out, gain_n, shift_n)
    return (new_nodes, new_coarse, new_edges)


def solution(mesh):
    regions, groups = mesh.devices.shape
    fine = Mesh(mesh.devices.reshape(regions, groups // 2, 2), ("region", "pair", "core"))
    every = ("region", "pair", "core")
    rows, flat, copied = P(every, None), P(every), P()
    return jax.shard_map(
        on_device,
        mesh=fine,
        in_specs=(rows, rows, rows, flat, flat, flat) + (copied,) * 8,
        out_specs=(rows, rows, rows),
        check_vma=False,
    )
```

```python
import functools

import jax
import jax.numpy as jnp
from jax import lax
from jax.experimental import pallas as pl
from jax.experimental.pallas import tpu as pltpu
from jax.sharding import Mesh, PartitionSpec as P

F32 = jnp.float32
BF16 = jnp.bfloat16
LANES = 128
OWNED = 2
FINE = 768
STEP = 6
MIB = 1024 * 1024


def dot(a, b):
    return jnp.dot(a, b, preferred_element_type=F32)


def silu(x):
    half = 0.5 * x
    return half + half * jnp.tanh(half)


def normed(output, gain, shift):
    center = output - jnp.mean(output, axis=-1, keepdims=True)
    spread = jnp.mean(center * center, axis=-1, keepdims=True)
    return center * lax.rsqrt(spread + 1e-05) * gain + shift


def columns_of(ids_ref, first, count):
    parts = []
    for k in range(count):
        row = ids_ref[pl.ds(first + k, 1), :].astype(F32)
        parts.append(jnp.broadcast_to(row, (LANES, LANES)).T)
    return jnp.concatenate(parts, axis=0)


def rows_of(ids_ref, first, count):
    return jnp.concatenate([ids_ref[pl.ds(first + k, 1), :] for k in range(count)], axis=1)


def pick_rows(column, width, offset=0):
    lane = lax.broadcasted_iota(jnp.int32, column.shape, 1).astype(F32)
    parts = [
        (column == lane + float(offset + k * LANES)).astype(F32).astype(BF16)
        for k in range(width // LANES)
    ]
    return jnp.concatenate(parts, axis=1)


def copies_kernel(coarse_ref, out_ref, rows):
    owned, latent = coarse_ref.shape
    coarse = coarse_ref[...].astype(F32)
    for q in range(latent // LANES):
        rows[q * owned : (q + 1) * owned, :] = coarse[:, q * LANES : (q + 1) * LANES]
    out_ref[...] = jnp.broadcast_to(rows[...].astype(BF16)[None], out_ref.shape)


def local_kernel(
    core_ref,
    counts_ref,
    senders_ref,
    receivers_ref,
    edges_ref,
    nodes_ref,
    w_edge_ref,
    w_recv_ref,
    out_ref,
    places_ref,
    *,
    peers,
):
    block = pl.program_id(0)
    shape = places_ref.shape
    per_block = shape[0] // counts_ref.shape[0] * LANES
    row = lax.broadcasted_iota(jnp.int32, shape, 0)
    slot = row * LANES + lax.broadcasted_iota(jnp.int32, shape, 1)
    end = jnp.zeros(shape, jnp.int32)
    for b in range(counts_ref.shape[0]):
        end = jnp.where(slot >= b * per_block, b * per_block + counts_ref[b], end)
    ident = senders_ref[...] - FINE
    side = ((ident >> 1) & 1) ^ core_ref[0]
    place = (side * OWNED + (ident & 1)) * peers + (ident >> 2)
    places_ref[...] = jnp.where((slot < end) & (ident >= 0), place, -1)

    slots = edges_ref.shape[0]
    chunks = slots // LANES
    recv = columns_of(receivers_ref, block * chunks, chunks)
    offered = dot(nodes_ref[...], w_recv_ref[...]).astype(BF16)
    total = dot(edges_ref[...], w_edge_ref[...])
    total += dot(pick_rows(recv, nodes_ref.shape[0]), offered)
    out_ref[...] = total.astype(BF16)


def edge_update(before, sent, edges, w_mid_ref, w_out_ref, gain_ref, shift_ref):
    hidden = silu(before.astype(F32) + dot(sent, w_mid_ref[...])).astype(BF16)
    change = normed(dot(hidden, w_out_ref[...]), gain_ref[...], shift_ref[...])
    return (edges.astype(F32) + change).astype(BF16)


def coarse_edge_kernel(
    core_ref,
    places,
    before_ref,
    edges_ref,
    table_ref,
    w_in_ref,
    w_out_ref,
    gain_ref,
    shift_ref,
    updated_ref,
    to_mine_ref,
    to_other_ref,
    edges,
    w_mid,
    w_out,
    table,
    spread_rows,
    updated,
    sent,
    sems,
):
    slot_count, latent = edges.shape
    chunks = slot_count // LANES
    half = table.shape[0] // 2
    peers = half // OWNED
    tiles = chunks // STEP
    tile = STEP * LANES

    def copy(src, dst, k):
        one = pltpu.make_async_copy(src, dst, sems.at[k])
        one.start()
        return one

    weights = copy(w_in_ref.at[pl.ds(latent, latent), :], w_mid, 2)
    inputs = []
    for t in range(tiles):
        rows = pl.ds(t * tile, tile)
        inputs.append(
            [
                copy(edges_ref.at[rows, :], edges.at[rows, :], 5 + 3 * t),
            ]
        )
        if t == 0:
            weights_out = copy(w_out_ref, w_out, 3)
    spread_rows[...] = table_ref[...].astype(F32)

    def fill_table(core):
        for side in range(2):
            for r in range(8):
                q, j = r // OWNED, r % OWNED
                first = side * half + j * peers
                table[first : first + peers, q * LANES : (q + 1) * LANES] = spread_rows[
                    pl.ds((side ^ core) * 8 * peers + r, peers, stride=8), :
                ].astype(BF16)

    for core in range(2):
        pl.when(core_ref[0] == core)(functools.partial(fill_table, core))
    for t in range(tiles):
        rows = slice(t * tile, (t + 1) * tile)
        column = columns_of(places, t * STEP, STEP)
        sent[rows, :] = dot(pick_rows(column, 2 * half), table[...]).astype(BF16)
    weights.wait()
    results = []
    for t in range(tiles):
        for one in inputs[t]:
            one.wait()
        if t == 0:
            weights_out.wait()
        rows = slice(t * tile, (t + 1) * tile)
        updated[rows, :] = edge_update(
            before_ref[rows, :], sent[rows, :], edges[rows, :], w_mid, w_out, gain_ref, shift_ref
        )
        results.append(
            copy(
                updated.at[pl.ds(t * tile, tile), :],
                updated_ref.at[pl.ds(t * tile, tile), :],
                6 + 3 * t,
            )
        )
    row = rows_of(places, 0, chunks)
    target = lax.broadcasted_iota(jnp.int32, (2 * half, slot_count), 0)
    total = dot((row == target).astype(F32).astype(BF16), updated[...])
    for i, ref in enumerate((to_mine_ref, to_other_ref)):
        for r in range(8):
            q, j = r // OWNED, r % OWNED
            first = i * half + j * peers
            spread_rows[pl.ds(r, peers, stride=8), :] = total[
                first : first + peers, q * LANES : (q + 1) * LANES
            ]
        ref[...] = spread_rows[: half * latent // LANES, :].astype(BF16)
    for one in results:
        one.wait()


def fine_edge_kernel(
    counts_ref,
    senders_ref,
    receivers_ref,
    before_ref,
    edges_ref,
    updated_ref,
    low_ref,
    nodes_ref,
    high_ref,
    w_mid_ref,
    w_out_ref,
    gain_ref,
    shift_ref,
    node_in_ref,
    node_out_ref,
    node_gain_ref,
    node_shift_ref,
    new_edges_ref,
    new_nodes_ref,
):
    block = pl.program_id(0)
    slots, latent = edges_ref.shape
    node_rows = nodes_ref.shape[0]
    block_size = new_nodes_ref.shape[0]
    chunks = slots // LANES
    fresh = []
    for k in range(0, chunks, STEP):
        rows = slice(k * LANES, (k + STEP) * LANES)
        column = columns_of(senders_ref, block * chunks + k, STEP)
        sent = (
            dot(pick_rows(column, node_rows), low_ref[...])
            + dot(pick_rows(column, node_rows, node_rows), nodes_ref[...])
            + dot(pick_rows(column, node_rows, 2 * node_rows), high_ref[...])
        ).astype(BF16)
        old = edges_ref[rows, :]
        new = edge_update(
            before_ref[rows, :], sent, old, w_mid_ref, w_out_ref, gain_ref, shift_ref
        )
        new = jnp.where(column[:, :1] < float(3 * node_rows), new, updated_ref[rows, :])
        slot = lax.broadcasted_iota(jnp.int32, (STEP * LANES, 1), 0) + k * LANES
        new = jnp.where(slot < counts_ref[block], new, old)
        new_edges_ref[rows, :] = new
        fresh.append(new)
    row = rows_of(receivers_ref, block * chunks, chunks)
    slot = lax.broadcasted_iota(jnp.int32, (1, slots), 1)
    row = jnp.where(slot < counts_ref[block], row, -1)
    target = lax.broadcasted_iota(jnp.int32, (block_size, slots), 0)
    pick = (row == target).astype(F32).astype(BF16)
    fine_sum = dot(pick, jnp.concatenate(fresh, axis=0)).astype(BF16)
    nodes = nodes_ref[pl.ds(pl.multiple_of(block * block_size, block_size), block_size), :]
    hidden = silu(dot(nodes, node_in_ref[:latent, :]) + dot(fine_sum, node_in_ref[latent:, :]))
    change = normed(
        dot(hidden.astype(BF16), node_out_ref[...]), node_gain_ref[...], node_shift_ref[...]
    )
    new_nodes_ref[...] = (nodes.astype(F32) + change).astype(BF16)


def coarse_kernel(
    parts_ref,
    coarse_ref,
    w_in_ref,
    w_out_ref,
    gain_ref,
    shift_ref,
    out_ref,
    rows,
    joined,
):
    owned, latent = coarse_ref.shape
    quarters = latent // LANES
    rows[...] = jnp.sum(parts_ref[...].astype(F32), axis=0)
    joined[...] = jnp.zeros(joined.shape, F32)
    coarse = coarse_ref[...].astype(F32)
    joined[:owned, :latent] = coarse
    for q in range(quarters):
        joined[:owned, latent + q * LANES : latent + (q + 1) * LANES] = rows[
            q * owned : (q + 1) * owned, :
        ]
    hidden = silu(dot(joined[...].astype(BF16), w_in_ref[...])).astype(BF16)
    change = normed(dot(hidden, w_out_ref[...]), gain_ref[...], shift_ref[...])
    out_ref[...] = (coarse + change[:owned, :]).astype(BF16)


def whole(shape):
    return pl.BlockSpec(shape, lambda *_: (0,) * len(shape))


def in_hbm(*arrays):
    return [pltpu.with_memory_space_constraint(a, pltpu.HBM) for a in arrays]


def coarse_edges(
    core, places, before, edges, table, edge_in, edge_out, gain, shift
):
    slot_count, latent = edges.shape
    flat = jax.ShapeDtypeStruct((table.shape[0] // 2, LANES), BF16)
    half = flat.shape[0] * flat.shape[1] // latent
    tiles = slot_count // (STEP * LANES)
    smem = pl.BlockSpec(memory_space=pltpu.SMEM)
    vmem, anywhere = pl.BlockSpec(memory_space=pltpu.VMEM), pl.BlockSpec(memory_space=pl.ANY)
    edges, edge_in, edge_out = in_hbm(edges, edge_in, edge_out)
    return pl.pallas_call(
        coarse_edge_kernel,
        in_specs=[smem, vmem, vmem, anywhere, vmem, anywhere, anywhere, vmem, vmem],
        out_specs=[anywhere, vmem, vmem],
        out_shape=[pltpu.HBM(edges.shape, BF16), flat, flat],
        scratch_shapes=[
            pltpu.VMEM(edges.shape, BF16),
            pltpu.VMEM((latent, latent), BF16),
            pltpu.VMEM((latent, latent), BF16),
            pltpu.VMEM((2 * half, latent), BF16),
            pltpu.VMEM(table.shape, F32),
            pltpu.VMEM(edges.shape, BF16),
            pltpu.VMEM(edges.shape, BF16),
            pltpu.SemaphoreType.DMA((4 + 3 * tiles,)),
        ],
        compiler_params=pltpu.CompilerParams(vmem_limit_bytes=40 * MIB),
        cost_estimate=pl.CostEstimate(flops=0, bytes_accessed=0, transcendentals=0),
        name="coarse_edges",
    )(core, places, before, edges, table, edge_in, edge_out, gain, shift)


def on_device(
    nodes,
    coarse,
    edges,
    senders,
    receivers,
    counts,
    edge_in,
    edge_out,
    edge_gain,
    edge_shift,
    node_in,
    node_out,
    node_gain,
    node_shift,
):
    node_rows, latent = nodes.shape
    owned = coarse.shape[0]
    blocks = counts.shape[0]
    slot_count = edges.shape[0]
    slots = slot_count // blocks
    regions = lax.axis_size("region")
    peers = regions * lax.axis_size("pair")
    core = lax.axis_index("core")
    smem = pl.BlockSpec(memory_space=pltpu.SMEM)
    gain_e, shift_e = edge_gain.reshape(1, latent), edge_shift.reshape(1, latent)
    gain_n, shift_n = node_gain.reshape(1, latent), node_shift.reshape(1, latent)
    swap = [(0, 1), (1, 0)]

    chunk = (owned * latent // LANES, LANES)
    copies = pl.pallas_call(
        copies_kernel,
        in_specs=[pl.BlockSpec(memory_space=pltpu.VMEM)],
        out_specs=pl.BlockSpec(memory_space=pltpu.VMEM),
        out_shape=jax.ShapeDtypeStruct((peers,) + chunk, BF16),
        scratch_shapes=[pltpu.VMEM(chunk, F32)],
        name="copies",
    )(coarse)
    table = lax.all_to_all(copies, ("region", "pair"), 0, 0, tiled=True)

    forward = [(i, (i + 1) % regions) for i in range(regions)]
    backward = [((i + 1) % regions, i) for i in range(regions)]
    low = lax.ppermute(nodes, "region", forward)
    high = lax.ppermute(nodes, "region", backward)

    send_grid = senders.reshape(-1, LANES)
    recv_grid = receivers.reshape(-1, LANES)
    row_block = pl.BlockSpec((slots, latent), lambda b: (b, 0))
    node_block = pl.BlockSpec((node_rows // blocks, latent), lambda b: (b, 0))

    def w_part(k):
        return pl.BlockSpec((latent, latent), lambda b: (k, 0))

    core = core.reshape(1)
    before, places = pl.pallas_call(
        functools.partial(local_kernel, peers=peers),
        grid=(blocks,),
        in_specs=[smem, smem, whole(send_grid.shape), whole(recv_grid.shape), row_block, node_block, w_part(0), w_part(2)],
        out_specs=[row_block, whole(send_grid.shape)],
        out_shape=[
            pltpu.VMEM((slot_count, latent), BF16),
            pltpu.VMEM(send_grid.shape, jnp.int32),
        ],
        compiler_params=pltpu.CompilerParams(vmem_limit_bytes=60 * MIB),
        cost_estimate=pl.CostEstimate(
            flops=2 * slot_count * latent * (2 * latent + LANES),
            bytes_accessed=6 * MIB,
            transcendentals=0,
        ),
        name="local",
    )(core, counts, send_grid, recv_grid, *in_hbm(edges, nodes, edge_in, edge_in))

    table, before = lax.optimization_barrier((table, before))
    table = lax.all_gather(table.reshape(-1, LANES), "core", axis=0, tiled=True)
    updated, to_mine, to_other = coarse_edges(
        core, places, before, edges, table, edge_in, edge_out, gain_e, shift_e
    )
    to_other, low, high = lax.optimization_barrier((to_other, low, high))
    arrived = lax.ppermute(to_other, "core", swap)
    chip_sum = (to_mine.astype(F32) + arrived.astype(F32)).astype(BF16)
    chip_sum, updated = lax.optimization_barrier((chip_sum, updated))
    parts = lax.all_to_all(
        chip_sum.reshape((peers,) + chunk), ("region", "pair"), 0, 0, tiled=True
    )

    new_edges, new_nodes = pl.pallas_call(
        fine_edge_kernel,
        grid=(blocks,),
        in_specs=[
            smem,
            whole(send_grid.shape),
            whole(recv_grid.shape),
            row_block,
            row_block,
            row_block,
            whole(nodes.shape),
            whole(nodes.shape),
            whole(nodes.shape),
            w_part(1),
            whole(edge_out.shape),
            whole(gain_e.shape),
            whole(gain_e.shape),
            whole(node_in.shape),
            whole(node_out.shape),
            whole(gain_n.shape),
            whole(gain_n.shape),
        ],
        out_specs=[row_block, node_block],
        out_shape=[
            jax.ShapeDtypeStruct(edges.shape, BF16),
            jax.ShapeDtypeStruct(nodes.shape, BF16),
        ],
        compiler_params=pltpu.CompilerParams(vmem_limit_bytes=60 * MIB),
        cost_estimate=pl.CostEstimate(
            flops=2 * slot_count * latent * (4 * latent + 2 * LANES),
            bytes_accessed=10 * MIB,
            transcendentals=slot_count * latent,
        ),
        name="fine_edges",
    )(
        counts,
        send_grid,
        recv_grid,
        before,
        edges,
        updated,
        low,
        nodes,
        high,
        edge_in,
        edge_out,
        gain_e,
        shift_e,
        node_in,
        node_out,
        gain_n,
        shift_n,
    )

    new_coarse = pl.pallas_call(
        coarse_kernel,
        in_specs=[pl.BlockSpec(memory_space=pltpu.VMEM)] * 6,
        out_specs=pl.BlockSpec(memory_space=pltpu.VMEM),
        out_shape=jax.ShapeDtypeStruct(coarse.shape, BF16),
        scratch_shapes=[pltpu.VMEM(chunk, F32), pltpu.VMEM((8, 2 * latent), F32)],
        compiler_params=pltpu.CompilerParams(vmem_limit_bytes=16 * MIB),
        name="coarse_nodes",
    )(parts, coarse, node_in, node_out, gain_n, shift_n)
    return (new_nodes, new_coarse, new_edges)


def solution(mesh):
    regions, groups = mesh.devices.shape
    fine = Mesh(mesh.devices.reshape(regions, groups // 2, 2), ("region", "pair", "core"))
    every = ("region", "pair", "core")
    rows, flat, copied = P(every, None), P(every), P()
    return jax.shard_map(
        on_device,
        mesh=fine,
        in_specs=(rows, rows, rows, flat, flat, flat) + (copied,) * 8,
        out_specs=(rows, rows, rows),
        check_vma=False,
    )
```

```python
import functools

import jax
import jax.numpy as jnp
from jax import lax
from jax.experimental import pallas as pl
from jax.experimental.pallas import tpu as pltpu
from jax.sharding import Mesh, PartitionSpec as P

F32 = jnp.float32
BF16 = jnp.bfloat16
LANES = 128
OWNED = 2
FINE = 768
STEP = 6
MIB = 1024 * 1024


def dot(a, b):
    return jnp.dot(a, b, preferred_element_type=F32)


def silu(x):
    half = 0.5 * x
    return half + half * jnp.tanh(half)


def normed(output, gain, shift):
    center = output - jnp.mean(output, axis=-1, keepdims=True)
    spread = jnp.mean(center * center, axis=-1, keepdims=True)
    return center * lax.rsqrt(spread + 1e-05) * gain + shift


def columns_of(ids_ref, first, count):
    parts = []
    for k in range(count):
        row = ids_ref[pl.ds(first + k, 1), :].astype(F32)
        parts.append(jnp.broadcast_to(row, (LANES, LANES)).T)
    return jnp.concatenate(parts, axis=0)


def rows_of(ids_ref, first, count):
    return jnp.concatenate([ids_ref[pl.ds(first + k, 1), :] for k in range(count)], axis=1)


def pick_rows(column, width, offset=0):
    lane = lax.broadcasted_iota(jnp.int32, column.shape, 1).astype(F32)
    parts = [
        (column == lane + float(offset + k * LANES)).astype(F32).astype(BF16)
        for k in range(width // LANES)
    ]
    return jnp.concatenate(parts, axis=1)


def local_kernel(
    core_ref,
    counts_ref,
    senders_ref,
    receivers_ref,
    edges_ref,
    nodes_ref,
    w_edge_ref,
    w_recv_ref,
    out_ref,
    places_ref,
    *,
    peers,
):
    block = pl.program_id(0)
    shape = places_ref.shape
    per_block = shape[0] // counts_ref.shape[0] * LANES
    row = lax.broadcasted_iota(jnp.int32, shape, 0)
    slot = row * LANES + lax.broadcasted_iota(jnp.int32, shape, 1)
    end = jnp.zeros(shape, jnp.int32)
    for b in range(counts_ref.shape[0]):
        end = jnp.where(slot >= b * per_block, b * per_block + counts_ref[b], end)
    ident = senders_ref[...] - FINE
    side = ((ident >> 1) & 1) ^ core_ref[0]
    place = (side * OWNED + (ident & 1)) * peers + (ident >> 2)
    places_ref[...] = jnp.where((slot < end) & (ident >= 0), place, -1)

    slots = edges_ref.shape[0]
    chunks = slots // LANES
    recv = columns_of(receivers_ref, block * chunks, chunks)
    offered = dot(nodes_ref[...], w_recv_ref[...]).astype(BF16)
    total = dot(edges_ref[...], w_edge_ref[...])
    total += dot(pick_rows(recv, nodes_ref.shape[0]), offered)
    out_ref[...] = total.astype(BF16)


def edge_update(before, sent, edges, w_mid_ref, w_out_ref, gain_ref, shift_ref):
    hidden = silu(before.astype(F32) + dot(sent, w_mid_ref[...])).astype(BF16)
    change = normed(dot(hidden, w_out_ref[...]), gain_ref[...], shift_ref[...])
    return (edges.astype(F32) + change).astype(BF16)


def coarse_edge_kernel(
    core_ref,
    places,
    before_ref,
    edges_ref,
    table_ref,
    w_in_ref,
    w_out_ref,
    gain_ref,
    shift_ref,
    updated_ref,
    to_mine_ref,
    to_other_ref,
    edges,
    w_mid,
    w_out,
    table,
    spread_rows,
    updated,
    sent,
    sems,
):
    slot_count, latent = edges.shape
    chunks = slot_count // LANES
    half = table.shape[0] // 2
    peers = half // OWNED
    tiles = chunks // STEP
    tile = STEP * LANES

    def copy(src, dst, k):
        one = pltpu.make_async_copy(src, dst, sems.at[k])
        one.start()
        return one

    weights = copy(w_in_ref.at[pl.ds(latent, latent), :], w_mid, 2)
    inputs = []
    for t in range(tiles):
        rows = pl.ds(t * tile, tile)
        inputs.append(
            [
                copy(edges_ref.at[rows, :], edges.at[rows, :], 5 + 3 * t),
            ]
        )
        if t == 0:
            weights_out = copy(w_out_ref, w_out, 3)
    spread_rows[: table_ref.shape[0], :] = table_ref[...].astype(F32)

    def fill_table(core):
        for side in range(2):
            for r in range(8):
                q, j = r // OWNED, r % OWNED
                first = side * half + j * peers
                table[first : first + peers, q * LANES : (q + 1) * LANES] = spread_rows[
                    pl.ds((side ^ core) * 8 * peers + r, peers, stride=8), :
                ].astype(BF16)

    for core in range(2):
        pl.when(core_ref[0] == core)(functools.partial(fill_table, core))
    for t in range(tiles):
        rows = slice(t * tile, (t + 1) * tile)
        column = columns_of(places, t * STEP, STEP)
        sent[rows, :] = dot(pick_rows(column, 2 * half), table[...]).astype(BF16)
    weights.wait()
    results = []
    for t in range(tiles):
        for one in inputs[t]:
            one.wait()
        if t == 0:
            weights_out.wait()
        rows = slice(t * tile, (t + 1) * tile)
        updated[rows, :] = edge_update(
            before_ref[rows, :], sent[rows, :], edges[rows, :], w_mid, w_out, gain_ref, shift_ref
        )
        results.append(
            copy(
                updated.at[pl.ds(t * tile, tile), :],
                updated_ref.at[pl.ds(t * tile, tile), :],
                6 + 3 * t,
            )
        )
    row = rows_of(places, 0, chunks)
    target = lax.broadcasted_iota(jnp.int32, (2 * half, slot_count), 0)
    total = dot((row == target).astype(F32).astype(BF16), updated[...])
    for i, ref in enumerate((to_mine_ref, to_other_ref)):
        for r in range(8):
            q, j = r // OWNED, r % OWNED
            first = i * half + j * peers
            spread_rows[pl.ds(r, peers, stride=8), :] = total[
                first : first + peers, q * LANES : (q + 1) * LANES
            ]
        ref[...] = spread_rows[: half * latent // LANES, :].astype(BF16)
    for one in results:
        one.wait()


def fine_edge_kernel(
    counts_ref,
    senders_ref,
    receivers_ref,
    before_ref,
    edges_ref,
    updated_ref,
    low_ref,
    nodes_ref,
    high_ref,
    w_mid_ref,
    w_out_ref,
    gain_ref,
    shift_ref,
    node_in_ref,
    node_out_ref,
    node_gain_ref,
    node_shift_ref,
    new_edges_ref,
    new_nodes_ref,
):
    block = pl.program_id(0)
    slots, latent = edges_ref.shape
    node_rows = nodes_ref.shape[0]
    block_size = new_nodes_ref.shape[0]
    chunks = slots // LANES
    fresh = []
    for k in range(0, chunks, STEP):
        rows = slice(k * LANES, (k + STEP) * LANES)
        column = columns_of(senders_ref, block * chunks + k, STEP)
        sent = (
            dot(pick_rows(column, node_rows), low_ref[...])
            + dot(pick_rows(column, node_rows, node_rows), nodes_ref[...])
            + dot(pick_rows(column, node_rows, 2 * node_rows), high_ref[...])
        ).astype(BF16)
        old = edges_ref[rows, :]
        new = edge_update(
            before_ref[rows, :], sent, old, w_mid_ref, w_out_ref, gain_ref, shift_ref
        )
        new = jnp.where(column[:, :1] < float(3 * node_rows), new, updated_ref[rows, :])
        slot = lax.broadcasted_iota(jnp.int32, (STEP * LANES, 1), 0) + k * LANES
        new = jnp.where(slot < counts_ref[block], new, old)
        new_edges_ref[rows, :] = new
        fresh.append(new)
    row = rows_of(receivers_ref, block * chunks, chunks)
    slot = lax.broadcasted_iota(jnp.int32, (1, slots), 1)
    row = jnp.where(slot < counts_ref[block], row, -1)
    target = lax.broadcasted_iota(jnp.int32, (block_size, slots), 0)
    pick = (row == target).astype(F32).astype(BF16)
    fine_sum = dot(pick, jnp.concatenate(fresh, axis=0)).astype(BF16)
    nodes = nodes_ref[pl.ds(pl.multiple_of(block * block_size, block_size), block_size), :]
    hidden = silu(dot(nodes, node_in_ref[:latent, :]) + dot(fine_sum, node_in_ref[latent:, :]))
    change = normed(
        dot(hidden.astype(BF16), node_out_ref[...]), node_gain_ref[...], node_shift_ref[...]
    )
    new_nodes_ref[...] = (nodes.astype(F32) + change).astype(BF16)


def coarse_kernel(
    parts_ref,
    coarse_ref,
    w_in_ref,
    w_out_ref,
    gain_ref,
    shift_ref,
    out_ref,
    rows,
    joined,
):
    owned, latent = coarse_ref.shape
    quarters = latent // LANES
    rows[...] = jnp.sum(parts_ref[...].astype(F32), axis=0)
    joined[...] = jnp.zeros(joined.shape, F32)
    coarse = coarse_ref[...].astype(F32)
    joined[:owned, :latent] = coarse
    for q in range(quarters):
        joined[:owned, latent + q * LANES : latent + (q + 1) * LANES] = rows[
            q * owned : (q + 1) * owned, :
        ]
    hidden = silu(dot(joined[...].astype(BF16), w_in_ref[...])).astype(BF16)
    change = normed(dot(hidden, w_out_ref[...]), gain_ref[...], shift_ref[...])
    out_ref[...] = (coarse + change[:owned, :]).astype(BF16)


def whole(shape):
    return pl.BlockSpec(shape, lambda *_: (0,) * len(shape))


def in_hbm(*arrays):
    return [pltpu.with_memory_space_constraint(a, pltpu.HBM) for a in arrays]


def coarse_edges(
    core, places, before, edges, table, edge_in, edge_out, gain, shift
):
    slot_count, latent = edges.shape
    flat = jax.ShapeDtypeStruct((table.shape[0] // 2, LANES), BF16)
    half = flat.shape[0] * flat.shape[1] // latent
    tiles = slot_count // (STEP * LANES)
    smem = pl.BlockSpec(memory_space=pltpu.SMEM)
    vmem, anywhere = pl.BlockSpec(memory_space=pltpu.VMEM), pl.BlockSpec(memory_space=pl.ANY)
    edges, edge_in, edge_out = in_hbm(edges, edge_in, edge_out)
    return pl.pallas_call(
        coarse_edge_kernel,
        in_specs=[smem, vmem, vmem, anywhere, vmem, anywhere, anywhere, vmem, vmem],
        out_specs=[anywhere, vmem, vmem],
        out_shape=[pltpu.HBM(edges.shape, BF16), flat, flat],
        scratch_shapes=[
            pltpu.VMEM(edges.shape, BF16),
            pltpu.VMEM((latent, latent), BF16),
            pltpu.VMEM((latent, latent), BF16),
            pltpu.VMEM((2 * half, latent), BF16),
            pltpu.VMEM((table.shape[0] + 8, LANES), F32),
            pltpu.VMEM(edges.shape, BF16),
            pltpu.VMEM(edges.shape, BF16),
            pltpu.SemaphoreType.DMA((4 + 3 * tiles,)),
        ],
        compiler_params=pltpu.CompilerParams(vmem_limit_bytes=40 * MIB),
        cost_estimate=pl.CostEstimate(flops=0, bytes_accessed=0, transcendentals=0),
        name="coarse_edges",
    )(core, places, before, edges, table, edge_in, edge_out, gain, shift)


def on_device(
    nodes,
    coarse,
    edges,
    senders,
    receivers,
    counts,
    edge_in,
    edge_out,
    edge_gain,
    edge_shift,
    node_in,
    node_out,
    node_gain,
    node_shift,
):
    node_rows, latent = nodes.shape
    owned = coarse.shape[0]
    blocks = counts.shape[0]
    slot_count = edges.shape[0]
    slots = slot_count // blocks
    regions = lax.axis_size("region")
    peers = regions * lax.axis_size("pair")
    core = lax.axis_index("core")
    smem = pl.BlockSpec(memory_space=pltpu.SMEM)
    gain_e, shift_e = edge_gain.reshape(1, latent), edge_shift.reshape(1, latent)
    gain_n, shift_n = node_gain.reshape(1, latent), node_shift.reshape(1, latent)
    swap = [(0, 1), (1, 0)]

    chunk = (owned * latent // LANES, LANES)
    small = coarse.reshape(owned, latent // LANES, LANES).transpose(1, 0, 2)
    copies = jnp.broadcast_to(small.reshape(1, *chunk), (peers,) + chunk)
    table = lax.all_to_all(copies, ("region", "pair"), 0, 0, tiled=True)

    forward = [(i, (i + 1) % regions) for i in range(regions)]
    backward = [((i + 1) % regions, i) for i in range(regions)]
    low = lax.ppermute(nodes, "region", forward)
    high = lax.ppermute(nodes, "region", backward)

    send_grid = senders.reshape(-1, LANES)
    recv_grid = receivers.reshape(-1, LANES)
    row_block = pl.BlockSpec((slots, latent), lambda b: (b, 0))
    node_block = pl.BlockSpec((node_rows // blocks, latent), lambda b: (b, 0))

    def w_part(k):
        return pl.BlockSpec((latent, latent), lambda b: (k, 0))

    core = core.reshape(1)
    before, places = pl.pallas_call(
        functools.partial(local_kernel, peers=peers),
        grid=(blocks,),
        in_specs=[smem, smem, whole(send_grid.shape), whole(recv_grid.shape), row_block, node_block, w_part(0), w_part(2)],
        out_specs=[row_block, whole(send_grid.shape)],
        out_shape=[
            pltpu.VMEM((slot_count, latent), BF16),
            pltpu.VMEM(send_grid.shape, jnp.int32),
        ],
        compiler_params=pltpu.CompilerParams(vmem_limit_bytes=60 * MIB),
        cost_estimate=pl.CostEstimate(
            flops=2 * slot_count * latent * (2 * latent + LANES),
            bytes_accessed=6 * MIB,
            transcendentals=0,
        ),
        name="local",
    )(core, counts, send_grid, recv_grid, *in_hbm(edges, nodes, edge_in, edge_in))

    table, before = lax.optimization_barrier((table, before))
    table = lax.all_gather(table.reshape(-1, LANES), "core", axis=0, tiled=True)
    updated, to_mine, to_other = coarse_edges(
        core, places, before, edges, table, edge_in, edge_out, gain_e, shift_e
    )
    to_other, low, high = lax.optimization_barrier((to_other, low, high))
    arrived = lax.ppermute(to_other, "core", swap)
    chip_sum = (to_mine.astype(F32) + arrived.astype(F32)).astype(BF16)
    chip_sum, updated = lax.optimization_barrier((chip_sum, updated))
    parts = lax.all_to_all(
        chip_sum.reshape((peers,) + chunk), ("region", "pair"), 0, 0, tiled=True
    )

    new_edges, new_nodes = pl.pallas_call(
        fine_edge_kernel,
        grid=(blocks,),
        in_specs=[
            smem,
            whole(send_grid.shape),
            whole(recv_grid.shape),
            row_block,
            row_block,
            row_block,
            whole(nodes.shape),
            whole(nodes.shape),
            whole(nodes.shape),
            w_part(1),
            whole(edge_out.shape),
            whole(gain_e.shape),
            whole(gain_e.shape),
            whole(node_in.shape),
            whole(node_out.shape),
            whole(gain_n.shape),
            whole(gain_n.shape),
        ],
        out_specs=[row_block, node_block],
        out_shape=[
            jax.ShapeDtypeStruct(edges.shape, BF16),
            jax.ShapeDtypeStruct(nodes.shape, BF16),
        ],
        compiler_params=pltpu.CompilerParams(vmem_limit_bytes=60 * MIB),
        cost_estimate=pl.CostEstimate(
            flops=2 * slot_count * latent * (4 * latent + 2 * LANES),
            bytes_accessed=10 * MIB,
            transcendentals=slot_count * latent,
        ),
        name="fine_edges",
    )(
        counts,
        send_grid,
        recv_grid,
        before,
        edges,
        updated,
        low,
        nodes,
        high,
        edge_in,
        edge_out,
        gain_e,
        shift_e,
        node_in,
        node_out,
        gain_n,
        shift_n,
    )

    new_coarse = pl.pallas_call(
        coarse_kernel,
        in_specs=[pl.BlockSpec(memory_space=pltpu.VMEM)] * 6,
        out_specs=pl.BlockSpec(memory_space=pltpu.VMEM),
        out_shape=jax.ShapeDtypeStruct(coarse.shape, BF16),
        scratch_shapes=[pltpu.VMEM(chunk, F32), pltpu.VMEM((8, 2 * latent), F32)],
        compiler_params=pltpu.CompilerParams(vmem_limit_bytes=16 * MIB),
        name="coarse_nodes",
    )(parts, coarse, node_in, node_out, gain_n, shift_n)
    return (new_nodes, new_coarse, new_edges)


def solution(mesh):
    regions, groups = mesh.devices.shape
    fine = Mesh(mesh.devices.reshape(regions, groups // 2, 2), ("region", "pair", "core"))
    every = ("region", "pair", "core")
    rows, flat, copied = P(every, None), P(every), P()
    return jax.shard_map(
        on_device,
        mesh=fine,
        in_specs=(rows, rows, rows, flat, flat, flat) + (copied,) * 8,
        out_specs=(rows, rows, rows),
        check_vma=False,
    )
```

```python
import functools

import jax
import jax.numpy as jnp
from jax import lax
from jax.experimental import pallas as pl
from jax.experimental.pallas import tpu as pltpu
from jax.sharding import Mesh, PartitionSpec as P

F32 = jnp.float32
BF16 = jnp.bfloat16
LANES = 128
OWNED = 2
FINE = 768
STEP = 6
MIB = 1024 * 1024


def dot(a, b):
    return jnp.dot(a, b, preferred_element_type=F32)


def silu(x):
    half = 0.5 * x
    return half + half * jnp.tanh(half)


def normed(output, gain, shift):
    center = output - jnp.mean(output, axis=-1, keepdims=True)
    spread = jnp.mean(center * center, axis=-1, keepdims=True)
    return center * lax.rsqrt(spread + 1e-05) * gain + shift


def columns_of(ids_ref, first, count):
    parts = []
    for k in range(count):
        row = ids_ref[pl.ds(first + k, 1), :].astype(F32)
        parts.append(jnp.broadcast_to(row, (LANES, LANES)).T)
    return jnp.concatenate(parts, axis=0)


def rows_of(ids_ref, first, count):
    return jnp.concatenate([ids_ref[pl.ds(first + k, 1), :] for k in range(count)], axis=1)


def pick_rows(column, width, offset=0):
    lane = lax.broadcasted_iota(jnp.int32, column.shape, 1).astype(F32)
    parts = [
        (column == lane + float(offset + k * LANES)).astype(F32).astype(BF16)
        for k in range(width // LANES)
    ]
    return jnp.concatenate(parts, axis=1)


def local_kernel(
    core_ref,
    counts_ref,
    senders_ref,
    receivers_ref,
    edges_ref,
    nodes_ref,
    w_edge_ref,
    w_recv_ref,
    out_ref,
    places_ref,
    *,
    peers,
):
    block = pl.program_id(0)
    shape = places_ref.shape
    per_block = shape[0] // counts_ref.shape[0] * LANES
    row = lax.broadcasted_iota(jnp.int32, shape, 0)
    slot = row * LANES + lax.broadcasted_iota(jnp.int32, shape, 1)
    end = jnp.zeros(shape, jnp.int32)
    for b in range(counts_ref.shape[0]):
        end = jnp.where(slot >= b * per_block, b * per_block + counts_ref[b], end)
    ident = senders_ref[...] - FINE
    side = ((ident >> 1) & 1) ^ core_ref[0]
    place = (side * OWNED + (ident & 1)) * peers + (ident >> 2)
    places_ref[...] = jnp.where((slot < end) & (ident >= 0), place, -1)

    slots = edges_ref.shape[0]
    chunks = slots // LANES
    recv = columns_of(receivers_ref, block * chunks, chunks)
    offered = dot(nodes_ref[...], w_recv_ref[...]).astype(BF16)
    total = dot(edges_ref[...], w_edge_ref[...])
    total += dot(pick_rows(recv, nodes_ref.shape[0]), offered)
    out_ref[...] = total.astype(BF16)


def edge_update(before, sent, edges, w_mid_ref, w_out_ref, gain_ref, shift_ref):
    hidden = silu(before.astype(F32) + dot(sent, w_mid_ref[...])).astype(BF16)
    change = normed(dot(hidden, w_out_ref[...]), gain_ref[...], shift_ref[...])
    return (edges.astype(F32) + change).astype(BF16)


def fill(core_ref, table_ref, spread_rows, table):
    half = table.shape[0] // 2
    peers = half // OWNED
    spread_rows[: table_ref.shape[0], :] = table_ref[...].astype(F32)

    def from_core(core):
        for side in range(2):
            for r in range(8):
                q, j = r // OWNED, r % OWNED
                first = side * half + j * peers
                table[first : first + peers, q * LANES : (q + 1) * LANES] = spread_rows[
                    pl.ds((side ^ core) * 8 * peers + r, peers, stride=8), :
                ].astype(BF16)

    for core in range(2):
        pl.when(core_ref[0] == core)(functools.partial(from_core, core))


def coarse_edge_kernel(
    core_ref,
    places,
    before_ref,
    edges_ref,
    table_ref,
    w_in_ref,
    w_out_ref,
    gain_ref,
    shift_ref,
    to_mine_ref,
    to_other_ref,
    edges,
    w_mid,
    w_out,
    table,
    spread_rows,
    updated,
    sent,
    sems,
):
    slot_count, latent = edges.shape
    chunks = slot_count // LANES
    half = table.shape[0] // 2
    peers = half // OWNED
    tiles = chunks // STEP
    tile = STEP * LANES

    def copy(src, dst, k):
        one = pltpu.make_async_copy(src, dst, sems.at[k])
        one.start()
        return one

    weights = copy(w_in_ref.at[pl.ds(latent, latent), :], w_mid, 2)
    inputs = []
    for t in range(tiles):
        rows = pl.ds(t * tile, tile)
        inputs.append(
            [
                copy(edges_ref.at[rows, :], edges.at[rows, :], 5 + 3 * t),
            ]
        )
        if t == 0:
            weights_out = copy(w_out_ref, w_out, 3)
    fill(core_ref, table_ref, spread_rows, table)
    for t in range(tiles):
        rows = slice(t * tile, (t + 1) * tile)
        column = columns_of(places, t * STEP, STEP)
        sent[rows, :] = dot(pick_rows(column, 2 * half), table[...]).astype(BF16)
    weights.wait()
    for t in range(tiles):
        for one in inputs[t]:
            one.wait()
        if t == 0:
            weights_out.wait()
        rows = slice(t * tile, (t + 1) * tile)
        updated[rows, :] = edge_update(
            before_ref[rows, :], sent[rows, :], edges[rows, :], w_mid, w_out, gain_ref, shift_ref
        )
    row = rows_of(places, 0, chunks)
    target = lax.broadcasted_iota(jnp.int32, (2 * half, slot_count), 0)
    total = dot((row == target).astype(F32).astype(BF16), updated[...])
    for i, ref in enumerate((to_mine_ref, to_other_ref)):
        for r in range(8):
            q, j = r // OWNED, r % OWNED
            first = i * half + j * peers
            spread_rows[pl.ds(r, peers, stride=8), :] = total[
                first : first + peers, q * LANES : (q + 1) * LANES
            ]
        ref[...] = spread_rows[: half * latent // LANES, :].astype(BF16)


def fine_edge_kernel(
    core_ref,
    counts_ref,
    places_ref,
    senders_ref,
    receivers_ref,
    before_ref,
    edges_ref,
    table_ref,
    low_ref,
    nodes_ref,
    high_ref,
    w_mid_ref,
    w_out_ref,
    gain_ref,
    shift_ref,
    node_in_ref,
    node_out_ref,
    node_gain_ref,
    node_shift_ref,
    new_edges_ref,
    new_nodes_ref,
    spread_rows,
    table,
):
    block = pl.program_id(0)
    slots, latent = edges_ref.shape
    node_rows = nodes_ref.shape[0]
    block_size = new_nodes_ref.shape[0]
    chunks = slots // LANES

    @pl.when(block == 0)
    def _():
        fill(core_ref, table_ref, spread_rows, table)

    fresh = []
    for k in range(0, chunks, STEP):
        rows = slice(k * LANES, (k + STEP) * LANES)
        column = columns_of(senders_ref, block * chunks + k, STEP)
        place = columns_of(places_ref, block * chunks + k, STEP)
        sent = (
            dot(pick_rows(place, table.shape[0]), table[...])
            + dot(pick_rows(column, node_rows), low_ref[...])
            + dot(pick_rows(column, node_rows, node_rows), nodes_ref[...])
            + dot(pick_rows(column, node_rows, 2 * node_rows), high_ref[...])
        ).astype(BF16)
        old = edges_ref[rows, :]
        new = edge_update(
            before_ref[rows, :], sent, old, w_mid_ref, w_out_ref, gain_ref, shift_ref
        )
        slot = lax.broadcasted_iota(jnp.int32, (STEP * LANES, 1), 0) + k * LANES
        new = jnp.where(slot < counts_ref[block], new, old)
        new_edges_ref[rows, :] = new
        fresh.append(new)
    row = rows_of(receivers_ref, block * chunks, chunks)
    slot = lax.broadcasted_iota(jnp.int32, (1, slots), 1)
    row = jnp.where(slot < counts_ref[block], row, -1)
    target = lax.broadcasted_iota(jnp.int32, (block_size, slots), 0)
    pick = (row == target).astype(F32).astype(BF16)
    fine_sum = dot(pick, jnp.concatenate(fresh, axis=0)).astype(BF16)
    nodes = nodes_ref[pl.ds(pl.multiple_of(block * block_size, block_size), block_size), :]
    hidden = silu(dot(nodes, node_in_ref[:latent, :]) + dot(fine_sum, node_in_ref[latent:, :]))
    change = normed(
        dot(hidden.astype(BF16), node_out_ref[...]), node_gain_ref[...], node_shift_ref[...]
    )
    new_nodes_ref[...] = (nodes.astype(F32) + change).astype(BF16)


def coarse_kernel(
    parts_ref,
    coarse_ref,
    w_in_ref,
    w_out_ref,
    gain_ref,
    shift_ref,
    out_ref,
    rows,
    joined,
):
    owned, latent = coarse_ref.shape
    quarters = latent // LANES
    rows[...] = jnp.sum(parts_ref[...].astype(F32), axis=0)
    joined[...] = jnp.zeros(joined.shape, F32)
    coarse = coarse_ref[...].astype(F32)
    joined[:owned, :latent] = coarse
    for q in range(quarters):
        joined[:owned, latent + q * LANES : latent + (q + 1) * LANES] = rows[
            q * owned : (q + 1) * owned, :
        ]
    hidden = silu(dot(joined[...].astype(BF16), w_in_ref[...])).astype(BF16)
    change = normed(dot(hidden, w_out_ref[...]), gain_ref[...], shift_ref[...])
    out_ref[...] = (coarse + change[:owned, :]).astype(BF16)


def whole(shape):
    return pl.BlockSpec(shape, lambda *_: (0,) * len(shape))


def in_hbm(*arrays):
    return [pltpu.with_memory_space_constraint(a, pltpu.HBM) for a in arrays]


def coarse_edges(
    core, places, before, edges, table, edge_in, edge_out, gain, shift
):
    slot_count, latent = edges.shape
    flat = jax.ShapeDtypeStruct((table.shape[0] // 2, LANES), BF16)
    half = flat.shape[0] * flat.shape[1] // latent
    tiles = slot_count // (STEP * LANES)
    smem = pl.BlockSpec(memory_space=pltpu.SMEM)
    vmem, anywhere = pl.BlockSpec(memory_space=pltpu.VMEM), pl.BlockSpec(memory_space=pl.ANY)
    edges, edge_in, edge_out = in_hbm(edges, edge_in, edge_out)
    return pl.pallas_call(
        coarse_edge_kernel,
        in_specs=[smem, vmem, vmem, anywhere, vmem, anywhere, anywhere, vmem, vmem],
        out_specs=[vmem, vmem],
        out_shape=[flat, flat],
        scratch_shapes=[
            pltpu.VMEM(edges.shape, BF16),
            pltpu.VMEM((latent, latent), BF16),
            pltpu.VMEM((latent, latent), BF16),
            pltpu.VMEM((2 * half, latent), BF16),
            pltpu.VMEM((table.shape[0] + 8, LANES), F32),
            pltpu.VMEM(edges.shape, BF16),
            pltpu.VMEM(edges.shape, BF16),
            pltpu.SemaphoreType.DMA((4 + 3 * tiles,)),
        ],
        compiler_params=pltpu.CompilerParams(vmem_limit_bytes=40 * MIB),
        cost_estimate=pl.CostEstimate(flops=0, bytes_accessed=0, transcendentals=0),
        name="coarse_edges",
    )(core, places, before, edges, table, edge_in, edge_out, gain, shift)


def on_device(
    nodes,
    coarse,
    edges,
    senders,
    receivers,
    counts,
    edge_in,
    edge_out,
    edge_gain,
    edge_shift,
    node_in,
    node_out,
    node_gain,
    node_shift,
):
    node_rows, latent = nodes.shape
    owned = coarse.shape[0]
    blocks = counts.shape[0]
    slot_count = edges.shape[0]
    slots = slot_count // blocks
    regions = lax.axis_size("region")
    peers = regions * lax.axis_size("pair")
    core = lax.axis_index("core")
    smem = pl.BlockSpec(memory_space=pltpu.SMEM)
    gain_e, shift_e = edge_gain.reshape(1, latent), edge_shift.reshape(1, latent)
    gain_n, shift_n = node_gain.reshape(1, latent), node_shift.reshape(1, latent)
    swap = [(0, 1), (1, 0)]

    chunk = (owned * latent // LANES, LANES)
    small = coarse.reshape(owned, latent // LANES, LANES).transpose(1, 0, 2)
    copies = jnp.broadcast_to(small.reshape(1, *chunk), (peers,) + chunk)
    table = lax.all_to_all(copies, ("region", "pair"), 0, 0, tiled=True)

    forward = [(i, (i + 1) % regions) for i in range(regions)]
    backward = [((i + 1) % regions, i) for i in range(regions)]
    low = lax.ppermute(nodes, "region", forward)
    high = lax.ppermute(nodes, "region", backward)

    send_grid = senders.reshape(-1, LANES)
    recv_grid = receivers.reshape(-1, LANES)
    row_block = pl.BlockSpec((slots, latent), lambda b: (b, 0))
    node_block = pl.BlockSpec((node_rows // blocks, latent), lambda b: (b, 0))

    def w_part(k):
        return pl.BlockSpec((latent, latent), lambda b: (k, 0))

    core = core.reshape(1)
    before, places = pl.pallas_call(
        functools.partial(local_kernel, peers=peers),
        grid=(blocks,),
        in_specs=[smem, smem, whole(send_grid.shape), whole(recv_grid.shape), row_block, node_block, w_part(0), w_part(2)],
        out_specs=[row_block, whole(send_grid.shape)],
        out_shape=[
            pltpu.VMEM((slot_count, latent), BF16),
            pltpu.VMEM(send_grid.shape, jnp.int32),
        ],
        compiler_params=pltpu.CompilerParams(vmem_limit_bytes=60 * MIB),
        cost_estimate=pl.CostEstimate(
            flops=2 * slot_count * latent * (2 * latent + LANES),
            bytes_accessed=6 * MIB,
            transcendentals=0,
        ),
        name="local",
    )(core, counts, send_grid, recv_grid, *in_hbm(edges, nodes, edge_in, edge_in))

    table, before = lax.optimization_barrier((table, before))
    table = lax.all_gather(table.reshape(-1, LANES), "core", axis=0, tiled=True)
    to_mine, to_other = coarse_edges(
        core, places, before, edges, table, edge_in, edge_out, gain_e, shift_e
    )
    to_other, low, high = lax.optimization_barrier((to_other, low, high))
    arrived = lax.ppermute(to_other, "core", swap)
    chip_sum = (to_mine.astype(F32) + arrived.astype(F32)).astype(BF16)
    chip_sum, before = lax.optimization_barrier((chip_sum, before))
    parts = lax.all_to_all(
        chip_sum.reshape((peers,) + chunk), ("region", "pair"), 0, 0, tiled=True
    )

    new_edges, new_nodes = pl.pallas_call(
        fine_edge_kernel,
        grid=(blocks,),
        in_specs=[
            smem,
            smem,
            whole(send_grid.shape),
            whole(send_grid.shape),
            whole(recv_grid.shape),
            row_block,
            row_block,
            whole(table.shape),
            whole(nodes.shape),
            whole(nodes.shape),
            whole(nodes.shape),
            w_part(1),
            whole(edge_out.shape),
            whole(gain_e.shape),
            whole(gain_e.shape),
            whole(node_in.shape),
            whole(node_out.shape),
            whole(gain_n.shape),
            whole(gain_n.shape),
        ],
        out_specs=[row_block, node_block],
        out_shape=[
            jax.ShapeDtypeStruct(edges.shape, BF16),
            jax.ShapeDtypeStruct(nodes.shape, BF16),
        ],
        scratch_shapes=[
            pltpu.VMEM((table.shape[0] + 8, LANES), F32),
            pltpu.VMEM((2 * peers * owned, latent), BF16),
        ],
        compiler_params=pltpu.CompilerParams(vmem_limit_bytes=60 * MIB),
        cost_estimate=pl.CostEstimate(
            flops=2 * slot_count * latent * (4 * latent + 2 * LANES),
            bytes_accessed=10 * MIB,
            transcendentals=slot_count * latent,
        ),
        name="fine_edges",
    )(
        core,
        counts,
        places,
        send_grid,
        recv_grid,
        before,
        edges,
        table,
        low,
        nodes,
        high,
        edge_in,
        edge_out,
        gain_e,
        shift_e,
        node_in,
        node_out,
        gain_n,
        shift_n,
    )

    new_coarse = pl.pallas_call(
        coarse_kernel,
        in_specs=[pl.BlockSpec(memory_space=pltpu.VMEM)] * 6,
        out_specs=pl.BlockSpec(memory_space=pltpu.VMEM),
        out_shape=jax.ShapeDtypeStruct(coarse.shape, BF16),
        scratch_shapes=[pltpu.VMEM(chunk, F32), pltpu.VMEM((8, 2 * latent), F32)],
        compiler_params=pltpu.CompilerParams(vmem_limit_bytes=16 * MIB),
        name="coarse_nodes",
    )(parts, coarse, node_in, node_out, gain_n, shift_n)
    return (new_nodes, new_coarse, new_edges)


def solution(mesh):
    regions, groups = mesh.devices.shape
    fine = Mesh(mesh.devices.reshape(regions, groups // 2, 2), ("region", "pair", "core"))
    every = ("region", "pair", "core")
    rows, flat, copied = P(every, None), P(every), P()
    return jax.shard_map(
        on_device,
        mesh=fine,
        in_specs=(rows, rows, rows, flat, flat, flat) + (copied,) * 8,
        out_specs=(rows, rows, rows),
        check_vma=False,
    )
```

```python
import functools

import jax
import jax.numpy as jnp
from jax import lax
from jax.experimental import pallas as pl
from jax.experimental.pallas import tpu as pltpu
from jax.sharding import Mesh, PartitionSpec as P

F32 = jnp.float32
BF16 = jnp.bfloat16
LANES = 128
OWNED = 2
FINE = 768
STEP = 6
MIB = 1024 * 1024


def dot(a, b):
    return jnp.dot(a, b, preferred_element_type=F32)


def silu(x):
    half = 0.5 * x
    return half + half * jnp.tanh(half)


def normed(output, gain, shift):
    center = output - jnp.mean(output, axis=-1, keepdims=True)
    spread = jnp.mean(center * center, axis=-1, keepdims=True)
    return center * lax.rsqrt(spread + 1e-05) * gain + shift


def columns_of(ids_ref, first, count):
    parts = []
    for k in range(count):
        row = ids_ref[pl.ds(first + k, 1), :].astype(F32)
        parts.append(jnp.broadcast_to(row, (LANES, LANES)).T)
    return jnp.concatenate(parts, axis=0)


def rows_of(ids_ref, first, count):
    return jnp.concatenate([ids_ref[pl.ds(first + k, 1), :] for k in range(count)], axis=1)


def pick_rows(column, width, offset=0):
    lane = lax.broadcasted_iota(jnp.int32, column.shape, 1).astype(F32)
    parts = [
        (column == lane + float(offset + k * LANES)).astype(F32).astype(BF16)
        for k in range(width // LANES)
    ]
    return jnp.concatenate(parts, axis=1)


def local_kernel(
    core_ref,
    counts_ref,
    senders_ref,
    receivers_ref,
    edges_ref,
    nodes_ref,
    w_edge_ref,
    w_recv_ref,
    out_ref,
    places_ref,
    *,
    peers,
):
    block = pl.program_id(0)
    shape = places_ref.shape
    per_block = shape[0] // counts_ref.shape[0] * LANES
    row = lax.broadcasted_iota(jnp.int32, shape, 0)
    slot = row * LANES + lax.broadcasted_iota(jnp.int32, shape, 1)
    end = jnp.zeros(shape, jnp.int32)
    for b in range(counts_ref.shape[0]):
        end = jnp.where(slot >= b * per_block, b * per_block + counts_ref[b], end)
    ident = senders_ref[...] - FINE
    side = ((ident >> 1) & 1) ^ core_ref[0]
    place = (side * OWNED + (ident & 1)) * peers + (ident >> 2)
    places_ref[...] = jnp.where((slot < end) & (ident >= 0), place, -1)

    slots = edges_ref.shape[0]
    chunks = slots // LANES
    recv = columns_of(receivers_ref, block * chunks, chunks)
    offered = dot(nodes_ref[...], w_recv_ref[...]).astype(BF16)
    total = dot(edges_ref[...], w_edge_ref[...])
    total += dot(pick_rows(recv, nodes_ref.shape[0]), offered)
    out_ref[...] = total.astype(BF16)


def edge_update(before, sent, edges, w_mid_ref, w_out_ref, gain_ref, shift_ref):
    hidden = silu(before.astype(F32) + dot(sent, w_mid_ref[...])).astype(BF16)
    change = normed(dot(hidden, w_out_ref[...]), gain_ref[...], shift_ref[...])
    return (edges.astype(F32) + change).astype(BF16)


def fill(core_ref, table_ref, spread_rows, table):
    half = table.shape[0] // 2
    peers = half // OWNED
    spread_rows[: table_ref.shape[0], :] = table_ref[...].astype(F32)

    def from_core(core):
        for side in range(2):
            for r in range(8):
                q, j = r // OWNED, r % OWNED
                first = side * half + j * peers
                table[first : first + peers, q * LANES : (q + 1) * LANES] = spread_rows[
                    pl.ds((side ^ core) * 8 * peers + r, peers, stride=8), :
                ].astype(BF16)

    for core in range(2):
        pl.when(core_ref[0] == core)(functools.partial(from_core, core))


def coarse_edge_kernel(
    core_ref,
    places,
    before_ref,
    edges_ref,
    table_ref,
    w_in_ref,
    w_out_ref,
    gain_ref,
    shift_ref,
    to_mine_ref,
    to_other_ref,
    edges,
    w_mid,
    w_out,
    table,
    spread_rows,
    updated,
    sent,
    sems,
):
    slot_count, latent = edges.shape
    chunks = slot_count // LANES
    half = table.shape[0] // 2
    peers = half // OWNED
    tiles = chunks // STEP
    tile = STEP * LANES

    def copy(src, dst, k):
        one = pltpu.make_async_copy(src, dst, sems.at[k])
        one.start()
        return one

    weights = copy(w_in_ref.at[pl.ds(latent, latent), :], w_mid, 2)
    inputs = []
    for t in range(tiles):
        rows = pl.ds(t * tile, tile)
        inputs.append(
            [
                copy(edges_ref.at[rows, :], edges.at[rows, :], 5 + 3 * t),
            ]
        )
        if t == 0:
            weights_out = copy(w_out_ref, w_out, 3)
    fill(core_ref, table_ref, spread_rows, table)
    for t in range(tiles):
        rows = slice(t * tile, (t + 1) * tile)
        column = columns_of(places, t * STEP, STEP)
        sent[rows, :] = dot(pick_rows(column, 2 * half), table[...]).astype(BF16)
    weights.wait()
    for t in range(tiles):
        for one in inputs[t]:
            one.wait()
        if t == 0:
            weights_out.wait()
        rows = slice(t * tile, (t + 1) * tile)
        updated[rows, :] = edge_update(
            before_ref[rows, :], sent[rows, :], edges[rows, :], w_mid, w_out, gain_ref, shift_ref
        )
    row = rows_of(places, 0, chunks)
    target = lax.broadcasted_iota(jnp.int32, (2 * half, slot_count), 0)
    total = dot((row == target).astype(F32).astype(BF16), updated[...])
    for i, ref in enumerate((to_mine_ref, to_other_ref)):
        for r in range(8):
            q, j = r // OWNED, r % OWNED
            first = i * half + j * peers
            spread_rows[pl.ds(r, peers, stride=8), :] = total[
                first : first + peers, q * LANES : (q + 1) * LANES
            ]
        ref[...] = spread_rows[: half * latent // LANES, :].astype(BF16)


def fine_edge_kernel(
    core_ref,
    counts_ref,
    places_ref,
    senders_ref,
    receivers_ref,
    before_ref,
    edges_ref,
    table_ref,
    low_ref,
    nodes_ref,
    high_ref,
    w_mid_ref,
    w_out_ref,
    gain_ref,
    shift_ref,
    coarse_ref,
    node_in_ref,
    node_out_ref,
    node_gain_ref,
    node_shift_ref,
    new_edges_ref,
    new_nodes_ref,
    begun_ref,
    spread_rows,
    table,
    padded,
):
    block = pl.program_id(0)
    slots, latent = edges_ref.shape
    node_rows = nodes_ref.shape[0]
    block_size = new_nodes_ref.shape[0]
    chunks = slots // LANES

    @pl.when(block == 0)
    def _():
        fill(core_ref, table_ref, spread_rows, table)
        padded[...] = jnp.zeros(padded.shape, F32)
        padded[: coarse_ref.shape[0], :] = coarse_ref[...].astype(F32)
        begun_ref[...] = dot(padded[...].astype(BF16), node_in_ref[:latent, :])

    fresh = []
    for k in range(0, chunks, STEP):
        rows = slice(k * LANES, (k + STEP) * LANES)
        column = columns_of(senders_ref, block * chunks + k, STEP)
        place = columns_of(places_ref, block * chunks + k, STEP)
        sent = (
            dot(pick_rows(place, table.shape[0]), table[...])
            + dot(pick_rows(column, node_rows), low_ref[...])
            + dot(pick_rows(column, node_rows, node_rows), nodes_ref[...])
            + dot(pick_rows(column, node_rows, 2 * node_rows), high_ref[...])
        ).astype(BF16)
        old = edges_ref[rows, :]
        new = edge_update(
            before_ref[rows, :], sent, old, w_mid_ref, w_out_ref, gain_ref, shift_ref
        )
        slot = lax.broadcasted_iota(jnp.int32, (STEP * LANES, 1), 0) + k * LANES
        new = jnp.where(slot < counts_ref[block], new, old)
        new_edges_ref[rows, :] = new
        fresh.append(new)
    row = rows_of(receivers_ref, block * chunks, chunks)
    slot = lax.broadcasted_iota(jnp.int32, (1, slots), 1)
    row = jnp.where(slot < counts_ref[block], row, -1)
    target = lax.broadcasted_iota(jnp.int32, (block_size, slots), 0)
    pick = (row == target).astype(F32).astype(BF16)
    fine_sum = dot(pick, jnp.concatenate(fresh, axis=0)).astype(BF16)
    nodes = nodes_ref[pl.ds(pl.multiple_of(block * block_size, block_size), block_size), :]
    hidden = silu(dot(nodes, node_in_ref[:latent, :]) + dot(fine_sum, node_in_ref[latent:, :]))
    change = normed(
        dot(hidden.astype(BF16), node_out_ref[...]), node_gain_ref[...], node_shift_ref[...]
    )
    new_nodes_ref[...] = (nodes.astype(F32) + change).astype(BF16)


def coarse_kernel(
    parts_ref,
    coarse_ref,
    begun_ref,
    w_in_ref,
    w_out_ref,
    gain_ref,
    shift_ref,
    out_ref,
    rows,
    joined,
):
    owned, latent = coarse_ref.shape
    quarters = latent // LANES
    rows[...] = jnp.sum(parts_ref[...].astype(F32), axis=0)
    joined[...] = jnp.zeros(joined.shape, F32)
    coarse = coarse_ref[...].astype(F32)
    for q in range(quarters):
        joined[:owned, q * LANES : (q + 1) * LANES] = rows[
            q * owned : (q + 1) * owned, :
        ]
    hidden = silu(begun_ref[...] + dot(joined[...].astype(BF16), w_in_ref[latent:, :])).astype(BF16)
    change = normed(dot(hidden, w_out_ref[...]), gain_ref[...], shift_ref[...])
    out_ref[...] = (coarse + change[:owned, :]).astype(BF16)


def whole(shape):
    return pl.BlockSpec(shape, lambda *_: (0,) * len(shape))


def in_hbm(*arrays):
    return [pltpu.with_memory_space_constraint(a, pltpu.HBM) for a in arrays]


def coarse_edges(
    core, places, before, edges, table, edge_in, edge_out, gain, shift
):
    slot_count, latent = edges.shape
    flat = jax.ShapeDtypeStruct((table.shape[0] // 2, LANES), BF16)
    half = flat.shape[0] * flat.shape[1] // latent
    tiles = slot_count // (STEP * LANES)
    smem = pl.BlockSpec(memory_space=pltpu.SMEM)
    vmem, anywhere = pl.BlockSpec(memory_space=pltpu.VMEM), pl.BlockSpec(memory_space=pl.ANY)
    edges, edge_in, edge_out = in_hbm(edges, edge_in, edge_out)
    return pl.pallas_call(
        coarse_edge_kernel,
        in_specs=[smem, vmem, vmem, anywhere, vmem, anywhere, anywhere, vmem, vmem],
        out_specs=[vmem, vmem],
        out_shape=[flat, flat],
        scratch_shapes=[
            pltpu.VMEM(edges.shape, BF16),
            pltpu.VMEM((latent, latent), BF16),
            pltpu.VMEM((latent, latent), BF16),
            pltpu.VMEM((2 * half, latent), BF16),
            pltpu.VMEM((table.shape[0] + 8, LANES), F32),
            pltpu.VMEM(edges.shape, BF16),
            pltpu.VMEM(edges.shape, BF16),
            pltpu.SemaphoreType.DMA((4 + 3 * tiles,)),
        ],
        compiler_params=pltpu.CompilerParams(vmem_limit_bytes=40 * MIB),
        cost_estimate=pl.CostEstimate(flops=0, bytes_accessed=0, transcendentals=0),
        name="coarse_edges",
    )(core, places, before, edges, table, edge_in, edge_out, gain, shift)


def on_device(
    nodes,
    coarse,
    edges,
    senders,
    receivers,
    counts,
    edge_in,
    edge_out,
    edge_gain,
    edge_shift,
    node_in,
    node_out,
    node_gain,
    node_shift,
):
    node_rows, latent = nodes.shape
    owned = coarse.shape[0]
    blocks = counts.shape[0]
    slot_count = edges.shape[0]
    slots = slot_count // blocks
    regions = lax.axis_size("region")
    peers = regions * lax.axis_size("pair")
    core = lax.axis_index("core")
    smem = pl.BlockSpec(memory_space=pltpu.SMEM)
    gain_e, shift_e = edge_gain.reshape(1, latent), edge_shift.reshape(1, latent)
    gain_n, shift_n = node_gain.reshape(1, latent), node_shift.reshape(1, latent)
    swap = [(0, 1), (1, 0)]

    chunk = (owned * latent // LANES, LANES)
    small = coarse.reshape(owned, latent // LANES, LANES).transpose(1, 0, 2)
    copies = jnp.broadcast_to(small.reshape(1, *chunk), (peers,) + chunk)
    table = lax.all_to_all(copies, ("region", "pair"), 0, 0, tiled=True)

    forward = [(i, (i + 1) % regions) for i in range(regions)]
    backward = [((i + 1) % regions, i) for i in range(regions)]
    low = lax.ppermute(nodes, "region", forward)
    high = lax.ppermute(nodes, "region", backward)

    send_grid = senders.reshape(-1, LANES)
    recv_grid = receivers.reshape(-1, LANES)
    row_block = pl.BlockSpec((slots, latent), lambda b: (b, 0))
    node_block = pl.BlockSpec((node_rows // blocks, latent), lambda b: (b, 0))

    def w_part(k):
        return pl.BlockSpec((latent, latent), lambda b: (k, 0))

    core = core.reshape(1)
    before, places = pl.pallas_call(
        functools.partial(local_kernel, peers=peers),
        grid=(blocks,),
        in_specs=[smem, smem, whole(send_grid.shape), whole(recv_grid.shape), row_block, node_block, w_part(0), w_part(2)],
        out_specs=[row_block, whole(send_grid.shape)],
        out_shape=[
            pltpu.VMEM((slot_count, latent), BF16),
            pltpu.VMEM(send_grid.shape, jnp.int32),
        ],
        compiler_params=pltpu.CompilerParams(vmem_limit_bytes=60 * MIB),
        cost_estimate=pl.CostEstimate(
            flops=2 * slot_count * latent * (2 * latent + LANES),
            bytes_accessed=6 * MIB,
            transcendentals=0,
        ),
        name="local",
    )(core, counts, send_grid, recv_grid, *in_hbm(edges, nodes, edge_in, edge_in))

    table, before = lax.optimization_barrier((table, before))
    table = lax.all_gather(table.reshape(-1, LANES), "core", axis=0, tiled=True)
    to_mine, to_other = coarse_edges(
        core, places, before, edges, table, edge_in, edge_out, gain_e, shift_e
    )
    to_other, low, high = lax.optimization_barrier((to_other, low, high))
    arrived = lax.ppermute(to_other, "core", swap)
    chip_sum = (to_mine.astype(F32) + arrived.astype(F32)).astype(BF16)
    chip_sum, before = lax.optimization_barrier((chip_sum, before))
    parts = lax.all_to_all(
        chip_sum.reshape((peers,) + chunk), ("region", "pair"), 0, 0, tiled=True
    )

    new_edges, new_nodes, begun = pl.pallas_call(
        fine_edge_kernel,
        grid=(blocks,),
        in_specs=[
            smem,
            smem,
            whole(send_grid.shape),
            whole(send_grid.shape),
            whole(recv_grid.shape),
            row_block,
            row_block,
            whole(table.shape),
            whole(nodes.shape),
            whole(nodes.shape),
            whole(nodes.shape),
            w_part(1),
            whole(edge_out.shape),
            whole(gain_e.shape),
            whole(gain_e.shape),
            whole(coarse.shape),
            whole(node_in.shape),
            whole(node_out.shape),
            whole(gain_n.shape),
            whole(gain_n.shape),
        ],
        out_specs=[row_block, node_block, whole((8, latent))],
        out_shape=[
            jax.ShapeDtypeStruct(edges.shape, BF16),
            jax.ShapeDtypeStruct(nodes.shape, BF16),
            jax.ShapeDtypeStruct((8, latent), F32),
        ],
        scratch_shapes=[
            pltpu.VMEM((table.shape[0] + 8, LANES), F32),
            pltpu.VMEM((2 * peers * owned, latent), BF16),
            pltpu.VMEM((8, latent), F32),
        ],
        compiler_params=pltpu.CompilerParams(vmem_limit_bytes=60 * MIB),
        cost_estimate=pl.CostEstimate(
            flops=2 * slot_count * latent * (4 * latent + 2 * LANES),
            bytes_accessed=10 * MIB,
            transcendentals=slot_count * latent,
        ),
        name="fine_edges",
    )(
        core,
        counts,
        places,
        send_grid,
        recv_grid,
        before,
        edges,
        table,
        low,
        nodes,
        high,
        edge_in,
        edge_out,
        gain_e,
        shift_e,
        coarse,
        node_in,
        node_out,
        gain_n,
        shift_n,
    )

    new_coarse = pl.pallas_call(
        coarse_kernel,
        in_specs=[pl.BlockSpec(memory_space=pltpu.VMEM)] * 7,
        out_specs=pl.BlockSpec(memory_space=pltpu.VMEM),
        out_shape=jax.ShapeDtypeStruct(coarse.shape, BF16),
        scratch_shapes=[pltpu.VMEM(chunk, F32), pltpu.VMEM((8, latent), F32)],
        compiler_params=pltpu.CompilerParams(vmem_limit_bytes=16 * MIB),
        name="coarse_nodes",
    )(parts, coarse, begun, node_in, node_out, gain_n, shift_n)
    return (new_nodes, new_coarse, new_edges)


def solution(mesh):
    regions, groups = mesh.devices.shape
    fine = Mesh(mesh.devices.reshape(regions, groups // 2, 2), ("region", "pair", "core"))
    every = ("region", "pair", "core")
    rows, flat, copied = P(every, None), P(every), P()
    return jax.shard_map(
        on_device,
        mesh=fine,
        in_specs=(rows, rows, rows, flat, flat, flat) + (copied,) * 8,
        out_specs=(rows, rows, rows),
        check_vma=False,
    )
```
